32 devices in a mesh: col: 16 (over z, x, core), tm: 2 (over y).
Axes of the slice: x: 2, y: 2, z: 4, core: 2. Of those that a mesh axis runs over, the one named last changes fastest.
Arguments:
- series: bfloat16 [1200, 24576], P(None, 'col'), may hold values from -700 to 700
- slab_series: float32 [1200, 512], P('tm', 'col'), may hold values from -700 to 700
- phase_index: int32 [4, 600], P(None, 'tm'), may hold values from 0 to 1199
Outputs:
- tile_peak: float32 [4, 512, 16], P(None, None, 'col')
- peak_all: float32 [4], replicated
The draws below stay inside these ranges and needn't reach their ends.
All inputs are finite; a program needn't handle non-finite values.
Results may differ from the reference program's by a relative error of at most 0.0013.
Values may be sent and summed in bfloat16 or wider, within the bound.
No kernel may reach another device: no remote copies, remote signals or barrier semaphores. Data moves between devices by JAX's collectives and lax.ppermute only.
A program may use at most 64 MiB of HBM per device.

```python
import math
import jax
import jax.numpy as jnp
from jax import lax

FRAMES = 1200
FREQS = 600
SURR = 4
COLS_DEV = 1536
VERTS = 24576
SLAB = 512
N_COL = 16


def rough_field(key, row_total, col_total):
    key_col, key_row, key_shift, key_noise = jax.random.split(key, 4)
    col_scale = jnp.exp(jax.random.uniform(key_col, (col_total,), jnp.float32, 0.0, math.log(10.0)))
    row_scale = jnp.exp(jax.random.uniform(key_row, (row_total,), jnp.float32, 0.0, math.log(10.0)))
    shift = jax.random.uniform(key_shift, (col_total,), jnp.float32, -2.0, 2.0)
    noise_field = jnp.clip(jax.random.normal(key_noise, (row_total, col_total), jnp.float32), -6.0, 6.0)
    return (noise_field * row_scale[:, None] + shift[None, :]) * col_scale[None, :]


def draw_series(key, part):
    return rough_field(jax.random.fold_in(key, 11), FRAMES, VERTS).astype(jnp.bfloat16)


def draw_slab_series(key, part):
    return rough_field(jax.random.fold_in(key, 23), FRAMES, SLAB).astype(jnp.float32)


def with_ends(result, key, least, top_value):
    longest = result.shape.index(max(result.shape))
    spots = []
    for shift in (0, 1):
        where = [jax.random.randint(jax.random.fold_in(key, axis), (), 0, length) for axis, length in enumerate(result.shape)]
        where[longest] = (where[longest] + shift) % result.shape[longest]
        spots.append(tuple(where))
    return result.at[spots[0]].set(least).at[spots[1]].set(top_value)


def setup_inputs(seed: int = 0) -> dict:
    key_of = jax.random.split(jax.random.key(seed), 4)
    return {
        "series": draw_series(jax.random.fold_in(key_of[3], 71), 0),
        "slab_series": draw_slab_series(jax.random.fold_in(key_of[3], 71), 0),
        "phase_index": with_ends(jax.random.randint(key_of[2], (SURR, FREQS), 0, FRAMES), jax.random.fold_in(key_of[2], 1), 0, FRAMES - 1).astype(jnp.int32),
    }


EPSILON = 1e-06
HIGHEST = lax.Precision.HIGHEST

def twiddle(frame_ids, freq_ids):
    turn_count = frame_ids[:, None] * freq_ids[None, :] % FRAMES
    angles = turn_count.astype(jnp.float32) * (2.0 * math.pi / FRAMES)
    return (jnp.cos(angles), jnp.sin(angles))

def rotate_back(spec_cos, spec_sin, phase_ids, freq_ids, cos_back, sin_back):
    phase_angle = phase_ids.astype(jnp.float32) * (2.0 * math.pi / FRAMES)
    phase_cos = jnp.cos(phase_angle)[:, :, None]
    phase_sin = jnp.sin(phase_angle)[:, :, None]
    weights = (jnp.where(freq_ids < FREQS, 2.0, 1.0) / FRAMES).astype(jnp.float32)[None, :, None]
    rot_real = (spec_cos[None] * phase_cos + spec_sin[None] * phase_sin) * weights
    rot_imag = (spec_cos[None] * phase_sin - spec_sin[None] * phase_cos) * weights
    return jnp.einsum('sfv,tf->svt', rot_real, cos_back, precision=HIGHEST) - jnp.einsum('sfv,tf->svt', rot_imag, sin_back, precision=HIGHEST)

def normalize_rows(surrogate):
    return (surrogate * lax.rsqrt(lax.optimization_barrier(jnp.sum(surrogate * surrogate, axis=2, keepdims=True)) + EPSILON)).astype(jnp.bfloat16)

def reference(series, slab_series, phase_index):
    frame_ids = jnp.arange(FRAMES, dtype=jnp.int32)
    freq_ids = jnp.arange(1, FREQS + 1, dtype=jnp.int32)
    cos_tab, sin_tab = twiddle(frame_ids, freq_ids)
    spec_cos = jnp.dot(cos_tab.T, slab_series, precision=HIGHEST)
    spec_sin = jnp.dot(sin_tab.T, slab_series, precision=HIGHEST)
    normed = normalize_rows(rotate_back(spec_cos, spec_sin, phase_index, freq_ids, cos_tab, sin_tab))
    normed_wide = normed.astype(jnp.float32)
    values = series.astype(jnp.float32)
    centered = values - lax.optimization_barrier(jnp.mean(values, axis=0, keepdims=True))
    normed_cols = (centered * lax.rsqrt(lax.optimization_barrier(jnp.sum(centered * centered, axis=0, keepdims=True)) + EPSILON)).astype(jnp.bfloat16)

    def block_peak(block_id):
        block_cols = lax.dynamic_slice_in_dim(normed_cols, block_id * COLS_DEV, COLS_DEV, 1).astype(jnp.float32)
        scores = jnp.einsum('srt,tc->src', normed_wide, block_cols)
        return lax.optimization_barrier(jnp.max(jnp.abs(scores), axis=2))
    blocks = lax.map(block_peak, jnp.arange(N_COL, dtype=jnp.int32))
    tile_peak = jnp.transpose(blocks, (1, 2, 0)) * math.sqrt(FRAMES)
    peak_all = lax.optimization_barrier(jnp.max(tile_peak, axis=(1, 2)))
    return (tile_peak, peak_all)
```

```python
import functools
import math

import jax
import jax.numpy as jnp
import ml_dtypes
import numpy as np
from jax import lax
from jax.experimental import pallas as pl
from jax.experimental.pallas import tpu as pltpu
from jax.sharding import Mesh, PartitionSpec as P

EPSILON = 1e-06
LANES = 128
CODE_TOP = 32767.0
VMEM = pl.BlockSpec(memory_space=pltpu.VMEM)


def round_up(value, unit):
    return -(-value // unit) * unit


def dft_tables(frames, freqs, n_tm):
    share = frames // n_tm
    share_pad = round_up(share, LANES)
    freq_pad = round_up(freqs, LANES)
    turns = np.arange(1, freqs + 1)[:, None] * np.arange(frames)[None, :] % frames
    angles = turns * (2.0 * math.pi / frames)
    table = np.zeros((2, freq_pad, n_tm, share_pad), np.float64)
    table[0, :freqs, :, :share] = np.cos(angles).reshape(freqs, n_tm, share)
    table[1, :freqs, :, :share] = np.sin(angles).reshape(freqs, n_tm, share)
    block_sums = table.sum(axis=3).transpose(2, 0, 1).reshape(n_tm, 1, 2 * freq_pad)
    table = table.reshape(2 * freq_pad, n_tm * share_pad)
    high = table.astype(ml_dtypes.bfloat16)
    low = (table - high.astype(np.float64)).astype(ml_dtypes.bfloat16)
    return high, low, block_sums.astype(np.float32)


def split_digits(value):
    scaled = value * 16.0
    first = scaled.astype(jnp.int32)
    rest = (scaled - first.astype(jnp.float32)) * 32768.0
    second = rest.astype(jnp.int32)
    third = ((rest - second.astype(jnp.float32)) * 32768.0).astype(jnp.int32)
    return first, second, third


def join_digits(first, second, third):
    return (
        first.astype(jnp.float32) * 2.0**-4
        + second.astype(jnp.float32) * 2.0**-19
        + third.astype(jnp.float32) * 2.0**-34
    )


def encode_kernel(share, slab_ref, code_ref):
    values = slab_ref[...]
    verts = values.shape[0]
    n_tm, n_grp, row_share, share_pad = code_ref.shape
    mean = jnp.sum(values, axis=1, keepdims=True) * (1.0 / share)
    offset = values - mean
    top = jnp.max(jnp.abs(offset), axis=1, keepdims=True)
    top_digits = split_digits(top)
    mean_digits = split_digits(mean)
    step = join_digits(*top_digits) * (1.0 / CODE_TOP)
    inverse = jnp.where(step > 0.0, 1.0 / jnp.where(step > 0.0, step, 1.0), 0.0)
    codes = jnp.clip(jnp.round(offset * inverse), -CODE_TOP, CODE_TOP).astype(jnp.int32)
    codes = jnp.concatenate(
        [codes, jnp.zeros((verts, share_pad - share), jnp.int32)], axis=1
    )
    lane = lax.broadcasted_iota(jnp.int32, (verts, share_pad), 1) - share
    for place, digit in enumerate(top_digits + mean_digits):
        codes = jnp.where(lane == place, digit, codes)
    for m in range(n_tm):
        block = codes[m * row_share : (m + 1) * row_share].astype(jnp.int16)
        for g in range(n_grp):
            code_ref[m, g] = block


def column_kernel(share, share_pad, series_ref, high_ref, low_ref, out_ref, normed_ref):
    values = series_ref[...].astype(jnp.float32)
    frames = values.shape[0]
    centered = values - jnp.sum(values, axis=0, keepdims=True) * (1.0 / frames)
    total = jnp.sum(centered * centered, axis=0, keepdims=True)
    normed = centered * lax.rsqrt(total + EPSILON)
    gap = share_pad - share
    for m in range(frames // share):
        normed_ref[pl.ds(m * share_pad, share), :] = normed[m * share : (m + 1) * share].astype(
            jnp.bfloat16
        )
        if gap:
            normed_ref[pl.ds(m * share_pad + share, gap), :] = jnp.zeros(
                (gap, values.shape[1]), jnp.bfloat16
            )
    tile = normed_ref[...]
    out = jnp.dot(high_ref[...], tile, preferred_element_type=jnp.float32)
    out += jnp.dot(low_ref[...], tile, preferred_element_type=jnp.float32)
    out_ref[...] = out.astype(jnp.bfloat16)


def dot_nt(left, right):
    return lax.dot_general(
        left, right, (((1,), (1,)), ((), ())), preferred_element_type=jnp.float32
    )


def score_kernel(
    sizes, code_ref, high_ref, low_ref, sums_ref, turn_ref, cols_ref, peak_ref, rot_ref
):
    share, frames, freqs, surr = sizes
    n_tm, rows, share_pad = code_ref.shape
    freq_pad = turn_ref.shape[1]
    spec = jnp.zeros((rows, 2 * freq_pad), jnp.float32)
    for m in range(n_tm):
        codes = code_ref[m].astype(jnp.int32)
        upper = ((codes + 128) >> 8) << 8
        lower = codes - upper
        upper = upper.astype(jnp.float32).astype(jnp.bfloat16)
        lower = lower.astype(jnp.float32).astype(jnp.bfloat16)
        digits = [codes[:, share + p : share + p + 1] for p in range(6)]
        step = join_digits(*digits[:3]) * (1.0 / CODE_TOP)
        mean = join_digits(*digits[3:])
        block = pl.ds(m * share_pad, share_pad)
        high = high_ref[:, block]
        part = dot_nt(upper, high) + dot_nt(lower, high) + dot_nt(upper, low_ref[:, block])
        spec = spec + part * step + mean * sums_ref[m]
    spec_cos = spec[:, :freq_pad]
    spec_sin = spec[:, freq_pad:]
    freq = lax.broadcasted_iota(jnp.int32, (1, freq_pad), 1)
    pair = jnp.where(freq < freqs - 1, (2.0 / frames) ** 2 * (frames / 2.0), 0.0)
    last = jnp.where(freq == freqs - 1, float(frames), 0.0)
    common = jnp.sum((spec_cos * spec_cos + spec_sin * spec_sin) * pair, axis=1, keepdims=True)
    inverse = []
    for s in range(surr):
        cos_row = turn_ref[pl.ds(s, 1), :]
        sin_row = turn_ref[pl.ds(surr + s, 1), :]
        rot_real = spec_cos * cos_row + spec_sin * sin_row
        rot_imag = spec_cos * sin_row - spec_sin * cos_row
        energy = common + jnp.sum(rot_real * rot_real * last, axis=1, keepdims=True)
        inverse.append(lax.rsqrt(energy + EPSILON) * math.sqrt(frames))
        span = pl.ds(s * rows, rows)
        rot_ref[span, :freq_pad] = rot_real.astype(jnp.bfloat16)
        rot_ref[span, freq_pad:] = (-rot_imag).astype(jnp.bfloat16)
    rot = rot_ref[...]
    width = cols_ref.shape[1]
    step_cols = 2 * LANES
    top = jnp.zeros((surr * rows, LANES), jnp.float32)
    for start in range(0, width, step_cols):
        scores = jnp.abs(
            jnp.dot(rot, cols_ref[:, pl.ds(start, step_cols)], preferred_element_type=jnp.float32)
        )
        for part in range(0, step_cols, LANES):
            top = jnp.maximum(top, scores[:, part : part + LANES])
    for s in range(surr):
        scaled = top[s * rows : (s + 1) * rows] * inverse[s]
        peak_ref[pl.ds(s, 1), :] = jnp.max(scaled.T, axis=0, keepdims=True)


def tm_exchange(value, n_tm):
    if n_tm == 2:
        other = lax.ppermute(value, "tm", [(0, 1), (1, 0)])
        first = lax.axis_index("tm") == 0
        return jnp.stack([jnp.where(first, value, other), jnp.where(first, other, value)])
    return lax.all_gather(value, "tm")


def body(dims, series, slab_series, phase_index):
    n_grp, n_lane, n_tm = dims
    frames, columns = series.shape
    share, verts = slab_series.shape
    surr = phase_index.shape[0]
    freqs = phase_index.shape[1] * n_tm
    row_share = verts // n_tm
    rows = n_grp * row_share
    share_pad = round_up(share, LANES)
    freq_pad = round_up(freqs, LANES)
    high, low, sums = (jnp.asarray(t) for t in dft_tables(frames, freqs, n_tm))

    codes = pl.pallas_call(
        functools.partial(encode_kernel, share),
        out_shape=jax.ShapeDtypeStruct((n_tm, n_grp, row_share, share_pad), jnp.int16),
        in_specs=[VMEM],
        out_specs=VMEM,
    )(slab_series.T)
    codes = codes.reshape(n_tm * n_grp, row_share, share_pad)
    received = lax.all_to_all(codes, ("tm", "grp"), 0, 0, tiled=True)

    phase = tm_exchange(phase_index, n_tm)
    phase = jnp.transpose(phase, (1, 0, 2)).reshape(surr, freqs)
    angle = phase.astype(jnp.float32) * (2.0 * math.pi / frames)
    weight = jnp.where(jnp.arange(1, freqs + 1) < freqs, 2.0, 1.0) / frames
    turn = jnp.concatenate([jnp.cos(angle) * weight, jnp.sin(angle) * weight], axis=0)
    turn = jnp.pad(turn, ((0, 0), (0, freq_pad - freqs)))

    tile = 2 * LANES
    cols = pl.pallas_call(
        functools.partial(column_kernel, share, share_pad),
        out_shape=jax.ShapeDtypeStruct((2 * freq_pad, columns), jnp.bfloat16),
        grid=(columns // tile,),
        in_specs=[pl.BlockSpec((frames, tile), lambda j: (0, j)), VMEM, VMEM],
        out_specs=pl.BlockSpec((2 * freq_pad, tile), lambda j: (0, j)),
        scratch_shapes=[pltpu.VMEM((n_tm * share_pad, tile), jnp.bfloat16)],
        compiler_params=pltpu.CompilerParams(vmem_limit_bytes=40 * 2**20),
    )(series, high, low)

    received, cols = lax.optimization_barrier((received, cols))
    lanes = [received]
    if n_lane == 2:
        lanes.append(lax.ppermute(received, "lane", [(0, 1), (1, 0)]))
    score = pl.pallas_call(
        functools.partial(score_kernel, (share, frames, freqs, surr)),
        out_shape=jax.ShapeDtypeStruct((surr, rows), jnp.float32),
        in_specs=[VMEM] * 6,
        out_specs=VMEM,
        scratch_shapes=[pltpu.VMEM((surr * rows, 2 * freq_pad), jnp.bfloat16)],
        compiler_params=pltpu.CompilerParams(vmem_limit_bytes=40 * 2**20),
    )
    peaks = [
        score(r.reshape(n_tm, rows, share_pad), high, low, sums, turn, cols) for r in lanes
    ]

    best = functools.reduce(jnp.maximum, peaks)
    n_dev = n_grp * n_lane * n_tm
    every = lax.all_to_all(
        jnp.broadcast_to(best, (n_dev, surr, rows)), ("grp", "lane", "tm"), 0, 0, tiled=True
    )
    peak_all = jnp.max(every, axis=(0, 2))

    if n_lane == 2:
        first = lax.axis_index("lane") == 0
        peaks = [jnp.where(first, peaks[0], peaks[1]), jnp.where(first, peaks[1], peaks[0])]
    own = jnp.stack(peaks)
    both = tm_exchange(own, n_tm).reshape(n_tm, n_lane, surr, n_grp, row_share)
    tile_peak = jnp.transpose(both, (2, 3, 1, 0, 4)).reshape(surr, -1, 1)
    return tile_peak, peak_all


def solution(mesh):
    n_col, n_tm = mesh.shape["col"], mesh.shape["tm"]
    n_lane = 2 if n_col % 2 == 0 else 1
    dims = (n_col // n_lane, n_lane, n_tm)
    split = Mesh(mesh.devices.reshape(dims), ("grp", "lane", "tm"))
    col = ("grp", "lane")
    return jax.shard_map(
        functools.partial(body, dims),
        mesh=split,
        in_specs=(P(None, col), P("tm", col), P(None, "tm")),
        out_specs=(P(None, None, col), P()),
        check_vma=False,
    )
```

```python
import functools
import math

import jax
import jax.numpy as jnp
import ml_dtypes
import numpy as np
from jax import lax
from jax.experimental import pallas as pl
from jax.experimental.pallas import tpu as pltpu
from jax.sharding import Mesh, PartitionSpec as P

EPSILON = 1e-06
LANES = 128
CODE_TOP = 32767.0
LOW_SCALE = 2.0**14
COARSE_SCALE = 2.0**6
COL_SCALE = 2.0**8
COL_REST_SCALE = LOW_SCALE * COL_SCALE / COARSE_SCALE
CODE_SCALE = COARSE_SCALE / LOW_SCALE
FLOAT8 = jnp.float8_e4m3fn
VMEM = pl.BlockSpec(memory_space=pltpu.VMEM)
HBM = pl.BlockSpec(memory_space=pltpu.HBM)
TILE = 2 * LANES


def round_up(value, unit):
    return -(-value // unit) * unit


def split_table(table, axis):
    high = table.astype(ml_dtypes.bfloat16)
    low = (table - high.astype(np.float64)) * LOW_SCALE
    low = np.concatenate([low, table * COARSE_SCALE], axis=axis).astype(ml_dtypes.float8_e4m3fn)
    return jnp.asarray(np.ascontiguousarray(high)), jnp.asarray(np.ascontiguousarray(low))


class Order:
    def __init__(self, freqs):
        self.half = round_up(-(-freqs // 2), 16)
        self.pad = round_up(2 * self.half, LANES)
        self.freq = np.zeros(self.pad, np.int64)
        self.freq[: freqs // 2] = np.arange(2, freqs + 1, 2)
        self.freq[self.half : self.half + freqs - freqs // 2] = np.arange(1, freqs + 1, 2)
        self.used = self.freq > 0

    def wave(self, points, frames):
        angles = (self.freq[:, None] * points[None, :] % frames) * (2.0 * math.pi / frames)
        return np.stack([np.cos(angles), np.sin(angles)]) * self.used[:, None]


def pad_last(array, size):
    return np.pad(array, [(0, 0)] * (array.ndim - 1) + [(0, size - array.shape[-1])])


def column_tables(frames, order):
    half_pad = round_up(frames // 2, LANES)
    wave = pad_last(order.wave(np.arange(frames // 2), frames), half_pad)[:, : 2 * order.half]
    wave = wave.reshape(2, 2, order.half, half_pad).transpose(1, 0, 2, 3)
    return split_table(wave.reshape(2, 2 * order.half, half_pad), 2)


def slab_tables(frames, share, n_tm, order):
    share_pad = round_up(share, LANES)
    wave = pad_last(order.wave(np.arange(share), frames), share_pad).transpose(0, 2, 1)
    high, low = split_table(wave, 1)
    sums = np.concatenate([wave[0].sum(axis=0), wave[1].sum(axis=0)])
    shift = order.wave(np.arange(n_tm) * share, frames).transpose(0, 2, 1)
    shift = np.concatenate([shift, shift], axis=2).reshape(2 * n_tm, 2 * order.pad)
    return high, low, jnp.asarray(np.concatenate([sums[None], shift]), jnp.float32)


def split_digits(value):
    scaled = value * 16.0
    first = scaled.astype(jnp.int32)
    rest = (scaled - first.astype(jnp.float32)) * 32768.0
    second = rest.astype(jnp.int32)
    third = ((rest - second.astype(jnp.float32)) * 32768.0).astype(jnp.int32)
    return first, second, third


def join_digits(first, second, third):
    return (
        first.astype(jnp.float32) * 2.0**-4
        + second.astype(jnp.float32) * 2.0**-19
        + third.astype(jnp.float32) * 2.0**-34
    )


def encode_kernel(share, slab_ref, code_ref):
    values = slab_ref[...]
    verts = values.shape[0]
    n_tm, n_grp, row_share, share_pad = code_ref.shape
    mean = jnp.sum(values, axis=1, keepdims=True) * (1.0 / share)
    offset = values - mean
    top = jnp.max(jnp.abs(offset), axis=1, keepdims=True)
    top_digits = split_digits(top)
    mean_digits = split_digits(mean)
    step = join_digits(*top_digits) * (1.0 / CODE_TOP)
    inverse = jnp.where(step > 0.0, 1.0 / jnp.where(step > 0.0, step, 1.0), 0.0)
    codes = jnp.clip(jnp.round(offset * inverse), -CODE_TOP, CODE_TOP).astype(jnp.int32)
    codes = jnp.concatenate(
        [codes, jnp.zeros((verts, share_pad - share), jnp.int32)], axis=1
    )
    lane = lax.broadcasted_iota(jnp.int32, (verts, share_pad), 1) - share
    for place, digit in enumerate(top_digits + mean_digits):
        codes = jnp.where(lane == place, digit, codes)
    for m in range(n_tm):
        block = codes[m * row_share : (m + 1) * row_share].astype(jnp.int16)
        for g in range(n_grp):
            code_ref[m, g] = block


def start_copy(source, target, sem):
    copy = pltpu.make_async_copy(source, target, sem)
    copy.start()
    return copy


def wait_all(copies):
    for copy in copies:
        copy.wait()


def column_kernel(
    series_hbm, high_hbm, low_hbm, out_hbm,
    series, high, low, out, normed_0, normed_1, coarse_0, coarse_1, load_sems, store_sems,
):
    n_tiles, frames, _ = series.shape
    half = frames // 2
    half_pad = high.shape[2]
    freq_half = high.shape[1] // 2
    freq_pad = out.shape[1] // 2
    gap = freq_pad - 2 * freq_half
    normed_refs, coarse_refs = (normed_0, normed_1), (coarse_0, coarse_1)

    def load_tile(j):
        return start_copy(series_hbm.at[:, pl.ds(j * TILE, TILE)], series.at[j], load_sems.at[j])

    tile_copies = [load_tile(0)]
    table_copies = [
        start_copy(high_hbm, high, load_sems.at[n_tiles]),
        start_copy(low_hbm, low, load_sems.at[n_tiles + 1]),
    ]
    tile_copies += [load_tile(j) for j in range(1, n_tiles)]

    def normalize(j):
        normed_ref, coarse_ref = normed_refs[j % 2], coarse_refs[j % 2]
        values = series[j].astype(jnp.float32)
        centered = values - jnp.sum(values, axis=0, keepdims=True) * (1.0 / frames)
        total = jnp.sum(centered * centered, axis=0, keepdims=True)
        normed = (centered * lax.rsqrt(total + EPSILON)).astype(jnp.bfloat16).astype(jnp.float32)
        first, second = normed[:half], normed[half:]
        for parity, part in enumerate((first + second, first - second)):
            if half_pad > half:
                part = jnp.concatenate([part, jnp.zeros((half_pad - half, TILE), jnp.float32)], axis=0)
            rounded = part.astype(jnp.bfloat16)
            rest = part - rounded.astype(jnp.float32)
            normed_ref[parity] = rounded
            coarse_ref[parity, pl.ds(0, half_pad), :] = (part * COL_SCALE).astype(FLOAT8)
            coarse_ref[parity, pl.ds(half_pad, half_pad), :] = (rest * COL_REST_SCALE).astype(FLOAT8)

    tile_copies[0].wait()
    normalize(0)
    wait_all(table_copies + tile_copies[1:2])
    stores = []
    for j in range(n_tiles):
        if j == 1:
            wait_all(tile_copies[2:])
        if j + 1 < n_tiles:
            normalize(j + 1)
        for parity in range(2):
            sums = jnp.dot(
                high[parity], normed_refs[j % 2][parity], preferred_element_type=jnp.float32
            )
            rest = jnp.dot(
                low[parity], coarse_refs[j % 2][parity], preferred_element_type=jnp.float32
            )
            sums = (sums + rest * (1.0 / (LOW_SCALE * COL_SCALE))).astype(jnp.bfloat16)
            for q in range(2):
                span = pl.ds(q * freq_pad + parity * freq_half, freq_half)
                out[j, span, :] = sums[q * freq_half : (q + 1) * freq_half]
        for q in range(2):
            if gap:
                span = pl.ds(q * freq_pad + 2 * freq_half, gap)
                out[j, span, :] = jnp.zeros((gap, TILE), jnp.bfloat16)
        stores.append(start_copy(out.at[j], out_hbm.at[j], store_sems.at[j]))
    wait_all(stores)


def spectrum_kernel(
    share, codes_hbm, high_hbm, low_hbm, cols_hbm, shift_ref, spec_ref, cols_ref,
    codes_ref, high, low, sems,
):
    n_tm, rows, share_pad = codes_ref.shape
    freq_pad = high.shape[2]
    codes_copy = start_copy(codes_hbm, codes_ref, sems.at[0])
    copies = [
        [
            start_copy(high_hbm.at[q], high.at[q], sems.at[1 + 2 * q]),
            start_copy(low_hbm.at[q], low.at[q], sems.at[2 + 2 * q]),
        ]
        for q in range(2)
    ]
    cols_copy = start_copy(cols_hbm.at[pl.ds(0, cols_ref.shape[0])], cols_ref, sems.at[5])
    codes_copy.wait()
    codes = codes_ref[...].reshape(n_tm * rows, share_pad).astype(jnp.int32)
    upper = ((codes + 128) >> 8) << 8
    lower = (codes - upper).astype(jnp.float32)
    upper = upper.astype(jnp.float32)
    coarse = jnp.concatenate([upper * CODE_SCALE, lower], axis=1).astype(FLOAT8)
    upper = upper.astype(jnp.bfloat16)
    digits = [codes[:, share + p : share + p + 1] for p in range(6)]
    step = join_digits(*digits[:3]) * (1.0 / CODE_TOP)
    mean = join_digits(*digits[3:])
    parts = []
    for q in range(2):
        wait_all(copies[q])
        part = jnp.dot(upper, high[q], preferred_element_type=jnp.float32)
        part += jnp.dot(coarse, low[q], preferred_element_type=jnp.float32) * (1.0 / COARSE_SCALE)
        part = part * step + mean * shift_ref[0:1, q * freq_pad : (q + 1) * freq_pad]
        if n_tm == 2:
            sign = shift_ref[2:3, :freq_pad]
            spec_ref[:, q * freq_pad : (q + 1) * freq_pad] = part[:rows] + part[rows:] * sign
        parts.append(part)
    if n_tm != 2:
        spec_cos = jnp.zeros((rows, freq_pad), jnp.float32)
        spec_sin = jnp.zeros((rows, freq_pad), jnp.float32)
        for m in range(n_tm):
            part_cos, part_sin = (part[m * rows : (m + 1) * rows] for part in parts)
            shift_cos = shift_ref[1 + m : 2 + m, :freq_pad]
            shift_sin = shift_ref[1 + n_tm + m : 2 + n_tm + m, :freq_pad]
            spec_cos += part_cos * shift_cos - part_sin * shift_sin
            spec_sin += part_sin * shift_cos + part_cos * shift_sin
        spec_ref[:, :freq_pad] = spec_cos
        spec_ref[:, freq_pad:] = spec_sin
    cols_copy.wait()


def rotate(frames, last_freq, spec_ref, turn_ref, rot_ref):
    rows = spec_ref.shape[0]
    surr, freq_pad = turn_ref.shape[0] // 2, turn_ref.shape[1]
    spec_cos = spec_ref[:, :freq_pad]
    spec_sin = spec_ref[:, freq_pad:]
    freq = lax.broadcasted_iota(jnp.int32, (1, freq_pad), 1)
    pair = jnp.where(freq != last_freq, (2.0 / frames) ** 2 * (frames / 2.0), 0.0)
    last = jnp.where(freq == last_freq, float(frames), 0.0)
    common = jnp.sum((spec_cos * spec_cos + spec_sin * spec_sin) * pair, axis=1, keepdims=True)
    scales = []
    for s in range(surr):
        cos_row = turn_ref[pl.ds(s, 1), :]
        sin_row = turn_ref[pl.ds(surr + s, 1), :]
        rot_real = spec_cos * cos_row + spec_sin * sin_row
        rot_imag = spec_cos * sin_row - spec_sin * cos_row
        energy = common + jnp.sum(rot_real * rot_real * last, axis=1, keepdims=True)
        scales.append(lax.rsqrt(energy + EPSILON) * math.sqrt(frames))
        span = pl.ds(s * rows, rows)
        rot_ref[span, :freq_pad] = rot_real.astype(jnp.bfloat16)
        rot_ref[span, freq_pad:] = (-rot_imag).astype(jnp.bfloat16)
    return scales


def raise_top(top, rot, cols_ref):
    for j in range(cols_ref.shape[0]):
        scores = jnp.abs(jnp.dot(rot, cols_ref[j], preferred_element_type=jnp.float32))
        for part in range(0, TILE, LANES):
            top = jnp.maximum(top, scores[:, part : part + LANES])
    return top


def row_peaks(top, scales):
    rows = scales[0].shape[0]
    peaks = [
        jnp.max((top[s * rows : (s + 1) * rows] * scale).T, axis=0, keepdims=True)
        for s, scale in enumerate(scales)
    ]
    return jnp.concatenate(peaks, axis=0)


def first_score_kernel(
    frames, last_freq, spec_ref, turn_ref, near_ref, cols_hbm, peak_ref, far_ref, rot_ref, sem
):
    n_near = near_ref.shape[0]
    copy = start_copy(cols_hbm.at[pl.ds(n_near, far_ref.shape[0])], far_ref, sem)
    scales = rotate(frames, last_freq, spec_ref, turn_ref, rot_ref)
    rot = rot_ref[...]
    top = raise_top(jnp.zeros((rot.shape[0], LANES), jnp.float32), rot, near_ref)
    copy.wait()
    peak_ref[...] = row_peaks(raise_top(top, rot, far_ref), scales)


def second_score_kernel(
    frames, last_freq, spec_ref, turn_ref, near_ref, far_ref, first_ref, own_ref, best_ref, rot_ref
):
    scales = rotate(frames, last_freq, spec_ref, turn_ref, rot_ref)
    rot = rot_ref[...]
    top = raise_top(jnp.zeros((rot.shape[0], LANES), jnp.float32), rot, near_ref)
    peaks = row_peaks(raise_top(top, rot, far_ref), scales)
    first = first_ref[...]
    own_ref[0] = first
    own_ref[1] = peaks
    best_ref[...] = jnp.broadcast_to(jnp.maximum(first, peaks)[None], best_ref.shape)


def tm_exchange(value, n_tm):
    if n_tm == 2:
        other = lax.ppermute(value, "tm", [(0, 1), (1, 0)])
        first = lax.axis_index("tm") == 0
        return jnp.stack([jnp.where(first, value, other), jnp.where(first, other, value)])
    return lax.all_gather(value, "tm")


def in_hbm(array):
    return pltpu.with_memory_space_constraint(array, pltpu.HBM)


def body(dims, series, slab_series, phase_index):
    n_grp, n_lane, n_tm = dims
    frames, columns = series.shape
    share, verts = slab_series.shape
    surr = phase_index.shape[0]
    freqs = phase_index.shape[1] * n_tm
    row_share = verts // n_tm
    rows = n_grp * row_share
    share_pad = round_up(share, LANES)
    half_pad = round_up(frames // 2, LANES)
    order = Order(freqs)
    last_freq = int(np.argmax(order.freq))
    points = 2 * order.pad
    limits = pltpu.CompilerParams(vmem_limit_bytes=24 * 2**20)

    codes = pl.pallas_call(
        functools.partial(encode_kernel, share),
        out_shape=jax.ShapeDtypeStruct((n_tm, n_grp, row_share, share_pad), jnp.int16),
        in_specs=[VMEM],
        out_specs=VMEM,
    )(slab_series.T)
    codes = codes.reshape(n_tm * n_grp, row_share, share_pad)
    received = lax.all_to_all(codes, ("tm", "grp"), 0, 0, tiled=True)

    phase = tm_exchange(phase_index, n_tm)
    phase = jnp.transpose(phase, (1, 0, 2)).reshape(surr, freqs)
    angle = phase.astype(jnp.float32) * (2.0 * math.pi / frames)
    weight = jnp.where(jnp.arange(1, freqs + 1) < freqs, 2.0, 1.0) / frames
    turn = jnp.concatenate([jnp.cos(angle) * weight, jnp.sin(angle) * weight], axis=0)
    gap = jnp.zeros((2 * surr, order.half - freqs // 2), jnp.float32)
    turn = jnp.concatenate([turn[:, 1::2], gap, turn[:, 0::2]], axis=1)
    turn = jnp.pad(turn, ((0, 0), (0, order.pad - turn.shape[1])))

    n_tiles = columns // TILE
    col_high, col_low = column_tables(frames, order)
    cols = pl.pallas_call(
        column_kernel,
        out_shape=pltpu.HBM((n_tiles, points, TILE), jnp.bfloat16),
        in_specs=[HBM] * 3,
        out_specs=HBM,
        scratch_shapes=[
            pltpu.VMEM((n_tiles, frames, TILE), jnp.bfloat16),
            pltpu.VMEM(col_high.shape, jnp.bfloat16),
            pltpu.VMEM(col_low.shape, FLOAT8),
            pltpu.VMEM((n_tiles, points, TILE), jnp.bfloat16),
        ]
        + [pltpu.VMEM((2, half_pad, TILE), jnp.bfloat16)] * 2
        + [pltpu.VMEM((2, 2 * half_pad, TILE), FLOAT8)] * 2
        + [pltpu.SemaphoreType.DMA((n_tiles + 2,)), pltpu.SemaphoreType.DMA((n_tiles,))],
        compiler_params=limits,
        cost_estimate=pl.CostEstimate(
            flops=6 * order.pad * frames * columns, transcendentals=0, bytes_accessed=0
        ),
    )(in_hbm(series), in_hbm(col_high), in_hbm(col_low))

    received, cols, turn = lax.optimization_barrier((received, cols, turn))
    high, low, shift = slab_tables(frames, share, n_tm, order)
    n_near = n_tiles // 2
    spec, near = pl.pallas_call(
        functools.partial(spectrum_kernel, share),
        out_shape=(
            jax.ShapeDtypeStruct((rows, points), jnp.float32),
            pltpu.VMEM((n_near, points, TILE), jnp.bfloat16),
        ),
        in_specs=[HBM] * 4 + [VMEM],
        out_specs=(VMEM, VMEM),
        scratch_shapes=[
            pltpu.VMEM((n_tm, rows, share_pad), jnp.int16),
            pltpu.VMEM(high.shape, jnp.bfloat16),
            pltpu.VMEM(low.shape, FLOAT8),
            pltpu.SemaphoreType.DMA((6,)),
        ],
        compiler_params=limits,
        cost_estimate=pl.CostEstimate(
            flops=4 * points * n_tm * share_pad * rows, transcendentals=0, bytes_accessed=0
        ),
    )(
        in_hbm(received.reshape(n_tm, rows, share_pad)),
        in_hbm(high), in_hbm(low), in_hbm(cols), shift,
    )
    other = lax.ppermute(spec, "lane", [(i, (i + 1) % n_lane) for i in range(n_lane)])
    score_cost = pl.CostEstimate(
        flops=2 * points * surr * rows * columns, transcendentals=0, bytes_accessed=0
    )
    rot_shape = pltpu.VMEM((surr * rows, points), jnp.bfloat16)
    first, far = pl.pallas_call(
        functools.partial(first_score_kernel, frames, last_freq),
        out_shape=(
            jax.ShapeDtypeStruct((surr, rows), jnp.float32),
            pltpu.VMEM((n_tiles - n_near, points, TILE), jnp.bfloat16),
        ),
        in_specs=[VMEM] * 3 + [HBM],
        out_specs=(VMEM, VMEM),
        scratch_shapes=[rot_shape, pltpu.SemaphoreType.DMA],
        compiler_params=limits,
        cost_estimate=score_cost,
    )(spec, turn, near, in_hbm(cols))
    n_dev = n_grp * n_lane * n_tm
    own, best = pl.pallas_call(
        functools.partial(second_score_kernel, frames, last_freq),
        out_shape=(
            jax.ShapeDtypeStruct((2, surr, rows), jnp.float32),
            jax.ShapeDtypeStruct((n_dev, surr, rows), jnp.float32),
        ),
        in_specs=[VMEM] * 5,
        out_specs=(VMEM, VMEM),
        scratch_shapes=[rot_shape],
        compiler_params=limits,
        cost_estimate=score_cost,
    )(other, turn, near, far, first)
    every = lax.all_to_all(best, ("grp", "lane", "tm"), 0, 0, tiled=True)
    peak_all = jnp.max(every, axis=(0, 2))

    own = jnp.where(lax.axis_index("lane") == 0, own, own[::-1])[:n_lane]
    both = tm_exchange(own, n_tm).reshape(n_tm, n_lane, surr, n_grp, row_share)
    tile_peak = jnp.transpose(both, (2, 3, 1, 0, 4)).reshape(surr, -1, 1)
    return tile_peak, peak_all


def solution(mesh):
    n_col, n_tm = mesh.shape["col"], mesh.shape["tm"]
    n_lane = 2 if n_col % 2 == 0 else 1
    dims = (n_col // n_lane, n_lane, n_tm)
    split = Mesh(mesh.devices.reshape(dims), ("grp", "lane", "tm"))
    col = ("grp", "lane")
    return jax.shard_map(
        functools.partial(body, dims),
        mesh=split,
        in_specs=(P(None, col), P("tm", col), P(None, "tm")),
        out_specs=(P(None, None, col), P()),
        check_vma=False,
    )
```

```python
import functools
import math

import jax
import jax.numpy as jnp
import ml_dtypes
import numpy as np
from jax import lax
from jax.experimental import pallas as pl
from jax.experimental.pallas import tpu as pltpu
from jax.sharding import Mesh, PartitionSpec as P

EPSILON = 1e-06
LANES = 128
CODE_TOP = 32767.0
LOW_SCALE = 2.0**14
COARSE_SCALE = 2.0**6
COL_SCALE = 2.0**8
COL_REST_SCALE = LOW_SCALE * COL_SCALE / COARSE_SCALE
CODE_SCALE = COARSE_SCALE / LOW_SCALE
FLOAT8 = jnp.float8_e4m3fn
VMEM = pl.BlockSpec(memory_space=pltpu.VMEM)
HBM = pl.BlockSpec(memory_space=pltpu.HBM)
TILE = 2 * LANES


def round_up(value, unit):
    return -(-value // unit) * unit


def split_table(table, axis):
    high = table.astype(ml_dtypes.bfloat16)
    low = (table - high.astype(np.float64)) * LOW_SCALE
    low = np.concatenate([low, table * COARSE_SCALE], axis=axis).astype(ml_dtypes.float8_e4m3fn)
    return jnp.asarray(np.ascontiguousarray(high)), jnp.asarray(np.ascontiguousarray(low))


class Order:
    def __init__(self, freqs):
        self.half = round_up(-(-freqs // 2), 16)
        self.pad = round_up(2 * self.half, LANES)
        self.freq = np.zeros(self.pad, np.int64)
        self.freq[: freqs // 2] = np.arange(2, freqs + 1, 2)
        self.freq[self.half : self.half + freqs - freqs // 2] = np.arange(1, freqs + 1, 2)
        self.used = self.freq > 0

    def wave(self, points, frames):
        angles = (self.freq[:, None] * points[None, :] % frames) * (2.0 * math.pi / frames)
        return np.stack([np.cos(angles), np.sin(angles)]) * self.used[:, None]


def pad_last(array, size):
    return np.pad(array, [(0, 0)] * (array.ndim - 1) + [(0, size - array.shape[-1])])


def column_tables(frames, order):
    half_pad = round_up(frames // 2, LANES)
    wave = pad_last(order.wave(np.arange(frames // 2), frames), half_pad)[:, : 2 * order.half]
    wave = wave.reshape(2, 2, order.half, half_pad).transpose(1, 0, 2, 3)
    return split_table(wave.reshape(2, 2 * order.half, half_pad), 2)


def slab_tables(frames, share, share_pad, n_tm, order):
    wave = pad_last(order.wave(np.arange(share), frames), share_pad).transpose(0, 2, 1)
    high, low = split_table(wave, 1)
    sums = np.concatenate([wave[0].sum(axis=0), wave[1].sum(axis=0)])
    shift = order.wave(np.arange(n_tm) * share, frames).transpose(0, 2, 1)
    shift = np.concatenate([shift, shift], axis=2).reshape(2 * n_tm, 2 * order.pad)
    return high, low, jnp.asarray(np.concatenate([sums[None], shift]), jnp.float32)


def placement(order, freqs, n_tm, rows):
    share = freqs // n_tm
    share_pad = round_up(share, rows)
    index = order.freq - 1
    row = index // share * share_pad + index % share
    table = np.zeros((n_tm * share_pad, order.pad), ml_dtypes.float8_e4m3fn)
    table[row[order.used], np.nonzero(order.used)[0]] = 1.0
    return jnp.asarray(table)


def split_digits(value):
    scaled = value * 16.0
    first = scaled.astype(jnp.int32)
    rest = (scaled - first.astype(jnp.float32)) * 32768.0
    second = rest.astype(jnp.int32)
    third = ((rest - second.astype(jnp.float32)) * 32768.0).astype(jnp.int32)
    return first, second, third


def join_digits(first, second, third):
    return (
        first.astype(jnp.float32) * 2.0**-4
        + second.astype(jnp.float32) * 2.0**-19
        + third.astype(jnp.float32) * 2.0**-34
    )


def phase_lane(share):
    return round_up(share + 6, 8)


def phase_chunks(freq_share, rows):
    return -(-freq_share // rows)


def encode_kernel(share, rows, slab_ref, phase_ref, code_ref):
    values = slab_ref[...]
    verts = values.shape[0]
    n_tm, n_grp, row_share, share_pad = code_ref.shape
    mean = jnp.sum(values, axis=1, keepdims=True) * (1.0 / share)
    offset = values - mean
    top = jnp.max(jnp.abs(offset), axis=1, keepdims=True)
    top_digits = split_digits(top)
    mean_digits = split_digits(mean)
    step = join_digits(*top_digits) * (1.0 / CODE_TOP)
    inverse = jnp.where(step > 0.0, 1.0 / jnp.where(step > 0.0, step, 1.0), 0.0)
    codes = jnp.clip(jnp.round(offset * inverse), -CODE_TOP, CODE_TOP).astype(jnp.int32)
    codes = jnp.concatenate(
        [codes, jnp.zeros((verts, share_pad - share), jnp.int32)], axis=1
    )
    lane = lax.broadcasted_iota(jnp.int32, (verts, share_pad), 1) - share
    for place, digit in enumerate(top_digits + mean_digits):
        codes = jnp.where(lane == place, digit, codes)

    surr, freq_share = phase_ref.shape
    chunks = phase_chunks(freq_share, rows)
    phase = phase_ref[...].astype(jnp.float32)
    phase = jnp.concatenate(
        [phase, jnp.zeros((surr, chunks * rows - freq_share), jnp.float32)], axis=1
    )
    phase = jnp.concatenate([phase[:, c * rows : (c + 1) * rows] for c in range(chunks)], axis=0)
    above = phase_lane(share) % LANES
    phase = jnp.concatenate(
        [
            jnp.zeros((above, rows), jnp.float32),
            phase,
            jnp.zeros((LANES - above - chunks * surr, rows), jnp.float32),
        ],
        axis=0,
    )
    phase = pltpu.roll(phase, rows - lax.axis_index("grp") * row_share, 1).T[:row_share]
    phase = jnp.concatenate([phase.astype(jnp.int32)] * n_tm, axis=0)
    edge = share_pad - LANES
    codes = jnp.concatenate([codes[:, :edge], codes[:, edge:] + phase], axis=1)
    for m in range(n_tm):
        block = codes[m * row_share : (m + 1) * row_share].astype(jnp.int16)
        for g in range(n_grp):
            code_ref[m, g] = block


def start_copy(source, target, sem):
    copy = pltpu.make_async_copy(source, target, sem)
    copy.start()
    return copy


def wait_all(copies):
    for copy in copies:
        copy.wait()


def column_kernel(
    series_hbm, high_hbm, low_hbm, out_hbm,
    series, high, low, out, normed_0, normed_1, coarse_0, coarse_1, load_sems, store_sems,
):
    n_tiles, frames, _ = series.shape
    half = frames // 2
    half_pad = high.shape[2]
    freq_half = high.shape[1] // 2
    freq_pad = out.shape[1] // 2
    gap = freq_pad - 2 * freq_half
    normed_refs, coarse_refs = (normed_0, normed_1), (coarse_0, coarse_1)

    def load_tile(j):
        return start_copy(series_hbm.at[:, pl.ds(j * TILE, TILE)], series.at[j], load_sems.at[j])

    tile_copies = [load_tile(0)]
    table_copies = [
        start_copy(high_hbm, high, load_sems.at[n_tiles]),
        start_copy(low_hbm, low, load_sems.at[n_tiles + 1]),
    ]
    tile_copies += [load_tile(j) for j in range(1, n_tiles)]

    def normalize(j):
        normed_ref, coarse_ref = normed_refs[j % 2], coarse_refs[j % 2]
        values = series[j].astype(jnp.float32)
        centered = values - jnp.sum(values, axis=0, keepdims=True) * (1.0 / frames)
        total = jnp.sum(centered * centered, axis=0, keepdims=True)
        normed = (centered * lax.rsqrt(total + EPSILON)).astype(jnp.bfloat16).astype(jnp.float32)
        first, second = normed[:half], normed[half:]
        for parity, part in enumerate((first + second, first - second)):
            if half_pad > half:
                part = jnp.concatenate([part, jnp.zeros((half_pad - half, TILE), jnp.float32)], axis=0)
            rounded = part.astype(jnp.bfloat16)
            rest = part - rounded.astype(jnp.float32)
            normed_ref[parity] = rounded
            coarse_ref[parity, pl.ds(0, half_pad), :] = (part * COL_SCALE).astype(FLOAT8)
            coarse_ref[parity, pl.ds(half_pad, half_pad), :] = (rest * COL_REST_SCALE).astype(FLOAT8)

    tile_copies[0].wait()
    normalize(0)
    wait_all(table_copies + tile_copies[1:2])
    stores = []
    for j in range(n_tiles):
        if j == 1:
            wait_all(tile_copies[2:])
        if j + 1 < n_tiles:
            normalize(j + 1)
        for parity in range(2):
            sums = jnp.dot(
                high[parity], normed_refs[j % 2][parity], preferred_element_type=jnp.float32
            )
            rest = jnp.dot(
                low[parity], coarse_refs[j % 2][parity], preferred_element_type=jnp.float32
            )
            sums = (sums + rest * (1.0 / (LOW_SCALE * COL_SCALE))).astype(jnp.bfloat16)
            for q in range(2):
                span = pl.ds(q * freq_pad + parity * freq_half, freq_half)
                out[j, span, :] = sums[q * freq_half : (q + 1) * freq_half]
        for q in range(2):
            if gap:
                span = pl.ds(q * freq_pad + 2 * freq_half, gap)
                out[j, span, :] = jnp.zeros((gap, TILE), jnp.bfloat16)
        stores.append(start_copy(out.at[j], out_hbm.at[j], store_sems.at[j]))
    wait_all(stores)


def surrogate_turns(frames, last_freq, phases, place_ref):
    surr = phases[0].shape[0]
    freq_pad = place_ref.shape[1]
    digits = []
    for phase in phases:
        parts = [phase >> 8, (phase >> 4) & 15, phase & 15]
        digits.append(jnp.concatenate(parts, axis=0).astype(jnp.float32))
    digits = jnp.concatenate(digits, axis=1).astype(FLOAT8)
    placed = jnp.dot(digits, place_ref[...], preferred_element_type=jnp.float32)
    angle = placed[:surr] * 256.0 + placed[surr : 2 * surr] * 16.0 + placed[2 * surr :]
    angle = angle * (2.0 * math.pi / frames)
    freq = lax.broadcasted_iota(jnp.int32, (1, freq_pad), 1)
    weight = jnp.where(freq == last_freq, 1.0 / frames, 2.0 / frames)
    return jnp.cos(angle) * weight, jnp.sin(angle) * weight


def rotate(frames, last_freq, spec_ref, turn_ref, rot_ref, scale_ref):
    rows = spec_ref.shape[0]
    surr, freq_pad = turn_ref.shape[0] // 2, turn_ref.shape[1]
    spec_cos = spec_ref[:, :freq_pad]
    spec_sin = spec_ref[:, freq_pad:]
    freq = lax.broadcasted_iota(jnp.int32, (1, freq_pad), 1)
    pair = jnp.where(freq != last_freq, (2.0 / frames) ** 2 * (frames / 2.0), 0.0)
    common = jnp.sum((spec_cos * spec_cos + spec_sin * spec_sin) * pair, axis=1, keepdims=True)
    block = last_freq // LANES * LANES
    last = jnp.where(freq[:, block : block + LANES] == last_freq, float(frames), 0.0)
    for s in range(surr):
        cos_row = turn_ref[pl.ds(s, 1), :]
        sin_row = turn_ref[pl.ds(surr + s, 1), :]
        rot_real = spec_cos * cos_row + spec_sin * sin_row
        rot_imag = spec_cos * sin_row - spec_sin * cos_row
        at_last = rot_real[:, block : block + LANES]
        energy = common + jnp.sum(at_last * at_last * last, axis=1, keepdims=True)
        scale_ref[:, s : s + 1] = lax.rsqrt(energy + EPSILON) * math.sqrt(frames)
        span = pl.ds(s * rows, rows)
        rot_ref[span, :freq_pad] = rot_real.astype(jnp.bfloat16)
        rot_ref[span, freq_pad:] = (-rot_imag).astype(jnp.bfloat16)


def spectrum_kernel(
    share, frames, last_freq, freq_share,
    codes_ref, high_hbm, low_hbm, place_hbm, cols_hbm, shift_ref,
    spec_ref, turn_ref, rot_ref, scale_ref, cols_ref,
    high, low, place, sems,
):
    n_tm, rows, share_pad = codes_ref.shape
    freq_pad = high.shape[2]
    copies = [
        [
            start_copy(high_hbm.at[q], high.at[q], sems.at[2 * q]),
            start_copy(low_hbm.at[q], low.at[q], sems.at[1 + 2 * q]),
        ]
        for q in range(2)
    ]
    place_copy = start_copy(place_hbm, place, sems.at[4])
    cols_copy = start_copy(cols_hbm.at[pl.ds(0, cols_ref.shape[0])], cols_ref, sems.at[5])
    codes = codes_ref[...].reshape(n_tm * rows, share_pad).astype(jnp.int32)
    upper = ((codes + 128) >> 8) << 8
    lower = (codes - upper).astype(jnp.float32)
    upper = upper.astype(jnp.float32)
    coarse = jnp.concatenate([upper * CODE_SCALE, lower], axis=1).astype(FLOAT8)
    upper = upper.astype(jnp.bfloat16)
    digits = [codes[:, share + p : share + p + 1] for p in range(6)]
    step = join_digits(*digits[:3]) * (1.0 / CODE_TOP)
    mean = join_digits(*digits[3:])
    parts = []
    for q in range(2):
        wait_all(copies[q])
        part = jnp.dot(upper, high[q], preferred_element_type=jnp.float32)
        part += jnp.dot(coarse, low[q], preferred_element_type=jnp.float32) * (1.0 / COARSE_SCALE)
        part = part * step + mean * shift_ref[0:1, q * freq_pad : (q + 1) * freq_pad]
        if n_tm == 2:
            sign = shift_ref[2:3, :freq_pad]
            spec_ref[:, q * freq_pad : (q + 1) * freq_pad] = part[:rows] + part[rows:] * sign
        parts.append(part)
    if n_tm != 2:
        spec_cos = jnp.zeros((rows, freq_pad), jnp.float32)
        spec_sin = jnp.zeros((rows, freq_pad), jnp.float32)
        for m in range(n_tm):
            part_cos, part_sin = (part[m * rows : (m + 1) * rows] for part in parts)
            shift_cos = shift_ref[1 + m : 2 + m, :freq_pad]
            shift_sin = shift_ref[1 + n_tm + m : 2 + n_tm + m, :freq_pad]
            spec_cos += part_cos * shift_cos - part_sin * shift_sin
            spec_sin += part_sin * shift_cos + part_cos * shift_sin
        spec_ref[:, :freq_pad] = spec_cos
        spec_ref[:, freq_pad:] = spec_sin
    surr = turn_ref.shape[0] // 2
    chunks = phase_chunks(freq_share, rows)
    above = phase_lane(share) % LANES
    phases = []
    for m in range(n_tm):
        block = codes[m * rows : (m + 1) * rows, share_pad - LANES :].astype(jnp.float32).T
        block = block[above : above + round_up(chunks * surr, 8)].astype(jnp.int32)
        parts = [block[c * surr : (c + 1) * surr] for c in range(chunks)]
        phases.append(jnp.concatenate(parts, axis=1))
    place_copy.wait()
    turn_cos, turn_sin = surrogate_turns(frames, last_freq, phases, place)
    turn_ref[pl.ds(0, surr), :] = turn_cos
    turn_ref[pl.ds(surr, surr), :] = turn_sin
    rotate(frames, last_freq, spec_ref, turn_ref, rot_ref, scale_ref)
    cols_copy.wait()


def raise_top(top, rot, cols_ref):
    for j in range(cols_ref.shape[0]):
        scores = jnp.abs(jnp.dot(rot, cols_ref[j], preferred_element_type=jnp.float32))
        for part in range(0, TILE, LANES):
            top = jnp.maximum(top, scores[:, part : part + LANES])
    return top


def row_peaks(top, scale_ref, surr):
    rows = scale_ref.shape[0]
    peaks = [
        jnp.max((top[s * rows : (s + 1) * rows] * scale_ref[:, s : s + 1]).T, axis=0, keepdims=True)
        for s in range(surr)
    ]
    return jnp.concatenate(peaks, axis=0)


def first_score_kernel(rot_ref, scale_ref, near_ref, cols_hbm, peak_ref, far_ref, sem):
    copy = start_copy(cols_hbm.at[pl.ds(near_ref.shape[0], far_ref.shape[0])], far_ref, sem)
    rot = rot_ref[...]
    top = raise_top(jnp.zeros((rot.shape[0], LANES), jnp.float32), rot, near_ref)
    copy.wait()
    peak_ref[...] = row_peaks(raise_top(top, rot, far_ref), scale_ref, peak_ref.shape[0])


def second_score_kernel(
    frames, last_freq, spec_ref, turn_ref, near_ref, far_ref, first_ref, own_ref, best_ref,
    rot_ref, scale_ref,
):
    rotate(frames, last_freq, spec_ref, turn_ref, rot_ref, scale_ref)
    rot = rot_ref[...]
    top = raise_top(jnp.zeros((rot.shape[0], LANES), jnp.float32), rot, near_ref)
    peaks = row_peaks(raise_top(top, rot, far_ref), scale_ref, first_ref.shape[0])
    first = first_ref[...]
    lane = lax.axis_index("lane")
    own_ref[lane] = first
    own_ref[1 - lane] = peaks
    best = jnp.max(jnp.maximum(first, peaks), axis=1, keepdims=True)
    lane_of = lax.broadcasted_iota(jnp.int32, (1, 1, best_ref.shape[2]), 2)
    row = jnp.zeros(lane_of.shape, jnp.float32)
    for s in range(best.shape[0]):
        row = jnp.where(lane_of == s, best[s : s + 1].reshape(1, 1, 1), row)
    best_ref[...] = jnp.broadcast_to(row, best_ref.shape)


def tm_exchange(value, n_tm):
    if n_tm == 2:
        other = lax.ppermute(value, "tm", [(0, 1), (1, 0)])
        first = lax.axis_index("tm") == 0
        return jnp.stack([jnp.where(first, value, other), jnp.where(first, other, value)])
    return lax.all_gather(value, "tm")


def in_hbm(array):
    return pltpu.with_memory_space_constraint(array, pltpu.HBM)


def body(dims, series, slab_series, phase_index):
    n_grp, n_lane, n_tm = dims
    frames, columns = series.shape
    share, verts = slab_series.shape
    surr = phase_index.shape[0]
    freqs = phase_index.shape[1] * n_tm
    row_share = verts // n_tm
    rows = n_grp * row_share
    share_pad = round_up(phase_lane(share) + phase_chunks(freqs // n_tm, rows) * surr, LANES)
    half_pad = round_up(frames // 2, LANES)
    order = Order(freqs)
    last_freq = int(np.argmax(order.freq))
    points = 2 * order.pad
    limits = pltpu.CompilerParams(vmem_limit_bytes=24 * 2**20)

    codes = pl.pallas_call(
        functools.partial(encode_kernel, share, rows),
        out_shape=jax.ShapeDtypeStruct((n_tm, n_grp, row_share, share_pad), jnp.int16),
        in_specs=[VMEM] * 2,
        out_specs=VMEM,
    )(slab_series.T, phase_index)
    codes = codes.reshape(n_tm * n_grp, row_share, share_pad)
    received = lax.all_to_all(codes, ("tm", "grp"), 0, 0, tiled=True)

    n_tiles = columns // TILE
    col_high, col_low = column_tables(frames, order)
    cols = pl.pallas_call(
        column_kernel,
        out_shape=pltpu.HBM((n_tiles, points, TILE), jnp.bfloat16),
        in_specs=[HBM] * 3,
        out_specs=HBM,
        scratch_shapes=[
            pltpu.VMEM((n_tiles, frames, TILE), jnp.bfloat16),
            pltpu.VMEM(col_high.shape, jnp.bfloat16),
            pltpu.VMEM(col_low.shape, FLOAT8),
            pltpu.VMEM((n_tiles, points, TILE), jnp.bfloat16),
        ]
        + [pltpu.VMEM((2, half_pad, TILE), jnp.bfloat16)] * 2
        + [pltpu.VMEM((2, 2 * half_pad, TILE), FLOAT8)] * 2
        + [pltpu.SemaphoreType.DMA((n_tiles + 2,)), pltpu.SemaphoreType.DMA((n_tiles,))],
        compiler_params=limits,
        cost_estimate=pl.CostEstimate(
            flops=6 * order.pad * frames * columns, transcendentals=0, bytes_accessed=0
        ),
    )(in_hbm(series), in_hbm(col_high), in_hbm(col_low))

    received, cols = lax.optimization_barrier((received, cols))
    high, low, shift = slab_tables(frames, share, share_pad, n_tm, order)
    place = placement(order, freqs, n_tm, rows)
    n_near = n_tiles // 2
    rot_shape = pltpu.VMEM((surr * rows, points), jnp.bfloat16)
    spec, turn, rot, scale, near = pl.pallas_call(
        functools.partial(spectrum_kernel, share, frames, last_freq, freqs // n_tm),
        out_shape=(
            jax.ShapeDtypeStruct((rows, points), jnp.float32),
            jax.ShapeDtypeStruct((2 * surr, order.pad), jnp.float32),
            rot_shape,
            jax.ShapeDtypeStruct((rows, surr), jnp.float32),
            pltpu.VMEM((n_near, points, TILE), jnp.bfloat16),
        ),
        in_specs=[VMEM] + [HBM] * 4 + [VMEM],
        out_specs=(VMEM,) * 5,
        scratch_shapes=[
            pltpu.VMEM(high.shape, jnp.bfloat16),
            pltpu.VMEM(low.shape, FLOAT8),
            pltpu.VMEM(place.shape, FLOAT8),
            pltpu.SemaphoreType.DMA((6,)),
        ],
        compiler_params=limits,
        cost_estimate=pl.CostEstimate(
            flops=4 * points * n_tm * share_pad * rows, transcendentals=0, bytes_accessed=0
        ),
    )(
        received.reshape(n_tm, rows, share_pad),
        in_hbm(high), in_hbm(low), in_hbm(place), in_hbm(cols), shift,
    )
    other = lax.ppermute(spec, "lane", [(i, (i + 1) % n_lane) for i in range(n_lane)])
    score_cost = pl.CostEstimate(
        flops=2 * points * surr * rows * columns, transcendentals=0, bytes_accessed=0
    )
    first, far = pl.pallas_call(
        first_score_kernel,
        out_shape=(
            jax.ShapeDtypeStruct((surr, rows), jnp.float32),
            pltpu.VMEM((n_tiles - n_near, points, TILE), jnp.bfloat16),
        ),
        in_specs=[VMEM] * 3 + [HBM],
        out_specs=(VMEM, VMEM),
        scratch_shapes=[pltpu.SemaphoreType.DMA],
        compiler_params=limits,
        cost_estimate=score_cost,
    )(rot, scale, near, in_hbm(cols))
    n_dev = n_grp * n_lane * n_tm
    own, best = pl.pallas_call(
        functools.partial(second_score_kernel, frames, last_freq),
        out_shape=(
            jax.ShapeDtypeStruct((2, surr, rows), jnp.float32),
            jax.ShapeDtypeStruct((n_dev, 1, LANES), jnp.float32),
        ),
        in_specs=[VMEM] * 5,
        out_specs=(VMEM, VMEM),
        scratch_shapes=[rot_shape, pltpu.VMEM((rows, surr), jnp.float32)],
        compiler_params=limits,
        cost_estimate=score_cost,
    )(other, turn, near, far, first)
    every = lax.all_to_all(best, ("grp", "lane", "tm"), 0, 0, tiled=True)
    peak_all = jnp.max(every, axis=(0, 1))[:surr]

    both = tm_exchange(own[:n_lane], n_tm).reshape(n_tm, n_lane, surr, n_grp, row_share)
    tile_peak = jnp.transpose(both, (2, 3, 1, 0, 4)).reshape(surr, -1, 1)
    return tile_peak, peak_all


def solution(mesh):
    n_col, n_tm = mesh.shape["col"], mesh.shape["tm"]
    n_lane = 2 if n_col % 2 == 0 else 1
    dims = (n_col // n_lane, n_lane, n_tm)
    split = Mesh(mesh.devices.reshape(dims), ("grp", "lane", "tm"))
    col = ("grp", "lane")
    return jax.shard_map(
        functools.partial(body, dims),
        mesh=split,
        in_specs=(P(None, col), P("tm", col), P(None, "tm")),
        out_specs=(P(None, None, col), P()),
        check_vma=False,
    )
```

```python
import functools
import math

import jax
import jax.numpy as jnp
import ml_dtypes
import numpy as np
from jax import lax
from jax.experimental import pallas as pl
from jax.experimental.pallas import tpu as pltpu
from jax.sharding import Mesh, PartitionSpec as P

EPSILON = 1e-06
LANES = 128
CODE_TOP = 32767.0
LOW_SCALE = 2.0**14
COARSE_SCALE = 2.0**6
COL_SCALE = 2.0**8
COL_REST_SCALE = LOW_SCALE * COL_SCALE / COARSE_SCALE
CODE_SCALE = COARSE_SCALE / LOW_SCALE
FLOAT8 = jnp.float8_e4m3fn
VMEM = pl.BlockSpec(memory_space=pltpu.VMEM)
HBM = pl.BlockSpec(memory_space=pltpu.HBM)
TILE = 2 * LANES


def round_up(value, unit):
    return -(-value // unit) * unit


def split_table(table, axis):
    high = table.astype(ml_dtypes.bfloat16)
    low = (table - high.astype(np.float64)) * LOW_SCALE
    low = np.concatenate([low, table * COARSE_SCALE], axis=axis).astype(ml_dtypes.float8_e4m3fn)
    return jnp.asarray(np.ascontiguousarray(high)), jnp.asarray(np.ascontiguousarray(low))


class Order:
    def __init__(self, freqs):
        self.half = round_up(-(-freqs // 2), 16)
        self.pad = round_up(2 * self.half, LANES)
        self.freq = np.zeros(self.pad, np.int64)
        self.freq[: freqs // 2] = np.arange(2, freqs + 1, 2)
        self.freq[self.half : self.half + freqs - freqs // 2] = np.arange(1, freqs + 1, 2)
        self.used = self.freq > 0

    def wave(self, points, frames):
        angles = (self.freq[:, None] * points[None, :] % frames) * (2.0 * math.pi / frames)
        return np.stack([np.cos(angles), np.sin(angles)]) * self.used[:, None]


def pad_last(array, size):
    return np.pad(array, [(0, 0)] * (array.ndim - 1) + [(0, size - array.shape[-1])])


def column_tables(frames, order):
    half_pad = round_up(frames // 2, LANES)
    wave = pad_last(order.wave(np.arange(frames // 2), frames), half_pad)[:, : 2 * order.half]
    wave = wave.reshape(2, 2, order.half, half_pad).transpose(1, 0, 2, 3)
    return split_table(wave.reshape(2, 2 * order.half, half_pad), 2)


def slab_tables(frames, share, share_pad, n_tm, order):
    wave = pad_last(order.wave(np.arange(share), frames), share_pad).transpose(0, 2, 1)
    high, low = split_table(wave, 1)
    sums = np.concatenate([wave[0].sum(axis=0), wave[1].sum(axis=0)])
    shift = order.wave(np.arange(n_tm) * share, frames).transpose(0, 2, 1)
    shift = np.concatenate([shift, shift], axis=2).reshape(2 * n_tm, 2 * order.pad)
    return high, low, jnp.asarray(np.concatenate([sums[None], shift]), jnp.float32)


def placement(order, freqs, n_tm, rows):
    share = freqs // n_tm
    share_pad = round_up(share, rows)
    index = order.freq - 1
    row = index // share * share_pad + index % share
    table = np.zeros((n_tm * share_pad, order.pad), ml_dtypes.float8_e4m3fn)
    table[row[order.used], np.nonzero(order.used)[0]] = 1.0
    return jnp.asarray(table)


def split_digits(value):
    scaled = value * 16.0
    first = scaled.astype(jnp.int32)
    rest = (scaled - first.astype(jnp.float32)) * 32768.0
    second = rest.astype(jnp.int32)
    third = ((rest - second.astype(jnp.float32)) * 32768.0).astype(jnp.int32)
    return first, second, third


def join_digits(first, second, third):
    return (
        first.astype(jnp.float32) * 2.0**-4
        + second.astype(jnp.float32) * 2.0**-19
        + third.astype(jnp.float32) * 2.0**-34
    )


def phase_lane(share):
    return round_up(share + 6, 8)


def phase_chunks(freq_share, rows):
    return -(-freq_share // rows)


def encode_kernel(share, rows, slab_ref, phase_ref, code_ref):
    values = slab_ref[...]
    verts = values.shape[0]
    n_tm, n_grp, row_share, share_pad = code_ref.shape
    mean = jnp.sum(values, axis=1, keepdims=True) * (1.0 / share)
    offset = values - mean
    top = jnp.max(jnp.abs(offset), axis=1, keepdims=True)
    top_digits = split_digits(top)
    mean_digits = split_digits(mean)
    step = join_digits(*top_digits) * (1.0 / CODE_TOP)
    inverse = jnp.where(step > 0.0, 1.0 / jnp.where(step > 0.0, step, 1.0), 0.0)
    codes = jnp.clip(jnp.round(offset * inverse), -CODE_TOP, CODE_TOP).astype(jnp.int32)
    codes = jnp.concatenate(
        [codes, jnp.zeros((verts, share_pad - share), jnp.int32)], axis=1
    )
    lane = lax.broadcasted_iota(jnp.int32, (verts, share_pad), 1) - share
    for place, digit in enumerate(top_digits + mean_digits):
        codes = jnp.where(lane == place, digit, codes)

    surr, freq_share = phase_ref.shape
    chunks = phase_chunks(freq_share, rows)
    phase = phase_ref[...].astype(jnp.float32)
    phase = jnp.concatenate(
        [phase, jnp.zeros((surr, chunks * rows - freq_share), jnp.float32)], axis=1
    )
    phase = jnp.concatenate([phase[:, c * rows : (c + 1) * rows] for c in range(chunks)], axis=0)
    above = phase_lane(share) % LANES
    phase = jnp.concatenate(
        [
            jnp.zeros((above, rows), jnp.float32),
            phase,
            jnp.zeros((LANES - above - chunks * surr, rows), jnp.float32),
        ],
        axis=0,
    )
    group = lax.axis_index("grp")
    place = jnp.where(lax.axis_index("lane") == 0, group, n_grp - 1 - group)
    phase = pltpu.roll(phase, rows - place * row_share, 1).T[:row_share]
    phase = jnp.concatenate([phase.astype(jnp.int32)] * n_tm, axis=0)
    edge = share_pad - LANES
    codes = jnp.concatenate([codes[:, :edge], codes[:, edge:] + phase], axis=1)
    for m in range(n_tm):
        block = codes[m * row_share : (m + 1) * row_share].astype(jnp.int16)
        for g in range(n_grp):
            code_ref[m, g] = block


def start_copy(source, target, sem):
    copy = pltpu.make_async_copy(source, target, sem)
    copy.start()
    return copy


def wait_all(copies):
    for copy in copies:
        copy.wait()


def column_kernel(
    series_hbm, high_hbm, low_hbm, out_hbm,
    series, high, low, out, normed_0, normed_1, coarse_0, coarse_1, load_sems, store_sems,
):
    n_tiles, frames, _ = series.shape
    half = frames // 2
    half_pad = high.shape[2]
    freq_half = high.shape[1] // 2
    freq_pad = out.shape[1] // 2
    gap = freq_pad - 2 * freq_half
    normed_refs, coarse_refs = (normed_0, normed_1), (coarse_0, coarse_1)

    def load_tile(j):
        return start_copy(series_hbm.at[:, pl.ds(j * TILE, TILE)], series.at[j], load_sems.at[j])

    tile_copies = [load_tile(0)]
    table_copies = [
        start_copy(high_hbm, high, load_sems.at[n_tiles]),
        start_copy(low_hbm, low, load_sems.at[n_tiles + 1]),
    ]
    tile_copies += [load_tile(j) for j in range(1, n_tiles)]

    def normalize(j):
        normed_ref, coarse_ref = normed_refs[j % 2], coarse_refs[j % 2]
        values = series[j].astype(jnp.float32)
        centered = values - jnp.sum(values, axis=0, keepdims=True) * (1.0 / frames)
        total = jnp.sum(centered * centered, axis=0, keepdims=True)
        normed = (centered * lax.rsqrt(total + EPSILON)).astype(jnp.bfloat16).astype(jnp.float32)
        first, second = normed[:half], normed[half:]
        for parity, part in enumerate((first + second, first - second)):
            if half_pad > half:
                part = jnp.concatenate([part, jnp.zeros((half_pad - half, TILE), jnp.float32)], axis=0)
            rounded = part.astype(jnp.bfloat16)
            rest = part - rounded.astype(jnp.float32)
            normed_ref[parity] = rounded
            coarse_ref[parity, pl.ds(0, half_pad), :] = (part * COL_SCALE).astype(FLOAT8)
            coarse_ref[parity, pl.ds(half_pad, half_pad), :] = (rest * COL_REST_SCALE).astype(FLOAT8)

    tile_copies[0].wait()
    normalize(0)
    wait_all(table_copies + tile_copies[1:2])
    stores = []
    for j in range(n_tiles):
        if j == 1:
            wait_all(tile_copies[2:])
        if j + 1 < n_tiles:
            normalize(j + 1)
        for parity in range(2):
            sums = jnp.dot(
                high[parity], normed_refs[j % 2][parity], preferred_element_type=jnp.float32
            )
            rest = jnp.dot(
                low[parity], coarse_refs[j % 2][parity], preferred_element_type=jnp.float32
            )
            sums = (sums + rest * (1.0 / (LOW_SCALE * COL_SCALE))).astype(jnp.bfloat16)
            for q in range(2):
                span = pl.ds(q * freq_pad + parity * freq_half, freq_half)
                out[j, span, :] = sums[q * freq_half : (q + 1) * freq_half]
        for q in range(2):
            if gap:
                span = pl.ds(q * freq_pad + 2 * freq_half, gap)
                out[j, span, :] = jnp.zeros((gap, TILE), jnp.bfloat16)
        stores.append(start_copy(out.at[j], out_hbm.at[j], store_sems.at[j]))
    wait_all(stores)


def surrogate_turns(frames, last_freq, phases, place_ref):
    surr = phases[0].shape[0]
    freq_pad = place_ref.shape[1]
    digits = []
    for phase in phases:
        parts = [phase >> 8, (phase >> 4) & 15, phase & 15]
        digits.append(jnp.concatenate(parts, axis=0).astype(jnp.float32))
    digits = jnp.concatenate(digits, axis=1).astype(FLOAT8)
    placed = jnp.dot(digits, place_ref[...], preferred_element_type=jnp.float32)
    turn = placed[:surr] * 256.0 + placed[surr : 2 * surr] * 16.0 + placed[2 * surr :]
    freq = lax.broadcasted_iota(jnp.int32, (1, freq_pad), 1)
    weight = jnp.where(freq == last_freq, 1.0 / frames, 2.0 / frames)
    cos, sin = turn_waves(frames, turn)
    return cos * weight, sin * weight


def turn_waves(frames, turn):
    quarter = frames / 4
    quadrant = jnp.floor(turn * (1.0 / quarter) + 0.5)
    x = (turn - quadrant * quarter) * (2.0 * math.pi / frames)
    y = x * x
    cos = 1.0 + y * (-1 / 2 + y * (1 / 24 + y * (-1 / 720 + y * (1 / 40320 - y * (1 / 3628800)))))
    sin = x * (1.0 + y * (-1 / 6 + y * (1 / 120 + y * (-1 / 5040 + y * (1 / 362880)))))
    odd = (quadrant == 1.0) | (quadrant == 3.0)
    left = (quadrant == 1.0) | (quadrant == 2.0)
    down = (quadrant == 2.0) | (quadrant == 3.0)
    near = jnp.where(odd, sin, cos)
    far = jnp.where(odd, cos, sin)
    return jnp.where(left, -near, near), jnp.where(down, -far, far)


def rotate(frames, last_freq, spec_ref, turn_ref, rot_ref, scale_ref):
    rows = spec_ref.shape[0]
    surr, freq_pad = turn_ref.shape[0] // 2, turn_ref.shape[1]
    spec_cos = spec_ref[:, :freq_pad]
    spec_sin = spec_ref[:, freq_pad:]
    freq = lax.broadcasted_iota(jnp.int32, (1, freq_pad), 1)
    pair = jnp.where(freq != last_freq, (2.0 / frames) ** 2 * (frames / 2.0), 0.0)
    common = jnp.sum((spec_cos * spec_cos + spec_sin * spec_sin) * pair, axis=1, keepdims=True)
    block = last_freq // LANES * LANES
    last = jnp.where(freq[:, block : block + LANES] == last_freq, float(frames), 0.0)
    for s in range(surr):
        cos_row = turn_ref[pl.ds(s, 1), :]
        sin_row = turn_ref[pl.ds(surr + s, 1), :]
        rot_real = spec_cos * cos_row + spec_sin * sin_row
        rot_imag = spec_cos * sin_row - spec_sin * cos_row
        at_last = rot_real[:, block : block + LANES]
        energy = common + jnp.sum(at_last * at_last * last, axis=1, keepdims=True)
        scale_ref[:, s : s + 1] = lax.rsqrt(energy + EPSILON) * math.sqrt(frames)
        span = pl.ds(s * rows, rows)
        rot_ref[span, :freq_pad] = rot_real.astype(jnp.bfloat16)
        rot_ref[span, freq_pad:] = (-rot_imag).astype(jnp.bfloat16)


def spectrum_kernel(
    share, frames, last_freq, freq_share,
    codes_ref, high_hbm, low_hbm, place_hbm, cols_hbm, shift_ref,
    spec_ref, turn_ref, cols_ref,
    high, low, place, sems,
):
    n_tm, rows, share_pad = codes_ref.shape
    freq_pad = high.shape[2]
    place_copy = start_copy(place_hbm, place, sems.at[4])
    copies = [
        [
            start_copy(high_hbm.at[q], high.at[q], sems.at[2 * q]),
            start_copy(low_hbm.at[q], low.at[q], sems.at[1 + 2 * q]),
        ]
        for q in range(2)
    ]
    cols_copy = start_copy(cols_hbm.at[pl.ds(0, cols_ref.shape[0])], cols_ref, sems.at[5])
    codes = codes_ref[...].reshape(n_tm * rows, share_pad).astype(jnp.int32)
    upper = ((codes + 128) >> 8) << 8
    lower = (codes - upper).astype(jnp.float32)
    upper = upper.astype(jnp.float32)
    coarse = jnp.concatenate([upper * CODE_SCALE, lower], axis=1).astype(FLOAT8)
    upper = upper.astype(jnp.bfloat16)
    digits = [codes[:, share + p : share + p + 1] for p in range(6)]
    step = join_digits(*digits[:3]) * (1.0 / CODE_TOP)
    mean = join_digits(*digits[3:])
    surr = turn_ref.shape[0] // 2
    chunks = phase_chunks(freq_share, rows)
    above = phase_lane(share) % LANES
    phases = []
    for m in range(n_tm):
        block = codes[m * rows : (m + 1) * rows, share_pad - LANES :].astype(jnp.float32).T
        block = block[above : above + round_up(chunks * surr, 8)].astype(jnp.int32)
        parts = [block[c * surr : (c + 1) * surr] for c in range(chunks)]
        phases.append(jnp.concatenate(parts, axis=1))
    place_copy.wait()
    turn_cos, turn_sin = surrogate_turns(frames, last_freq, phases, place)
    parts = []
    for q in range(2):
        wait_all(copies[q])
        part = jnp.dot(upper, high[q], preferred_element_type=jnp.float32)
        part += jnp.dot(coarse, low[q], preferred_element_type=jnp.float32) * (1.0 / COARSE_SCALE)
        part = part * step + mean * shift_ref[0:1, q * freq_pad : (q + 1) * freq_pad]
        if n_tm == 2:
            sign = shift_ref[2:3, :freq_pad]
            spec_ref[:, q * freq_pad : (q + 1) * freq_pad] = part[:rows] + part[rows:] * sign
        parts.append(part)
    if n_tm != 2:
        spec_cos = jnp.zeros((rows, freq_pad), jnp.float32)
        spec_sin = jnp.zeros((rows, freq_pad), jnp.float32)
        for m in range(n_tm):
            part_cos, part_sin = (part[m * rows : (m + 1) * rows] for part in parts)
            shift_cos = shift_ref[1 + m : 2 + m, :freq_pad]
            shift_sin = shift_ref[1 + n_tm + m : 2 + n_tm + m, :freq_pad]
            spec_cos += part_cos * shift_cos - part_sin * shift_sin
            spec_sin += part_sin * shift_cos + part_cos * shift_sin
        spec_ref[:, :freq_pad] = spec_cos
        spec_ref[:, freq_pad:] = spec_sin
    turn_ref[pl.ds(0, surr), :] = turn_cos
    turn_ref[pl.ds(surr, surr), :] = turn_sin
    cols_copy.wait()


def raise_top(top, rot, cols_ref):
    for j in range(cols_ref.shape[0]):
        scores = jnp.abs(jnp.dot(rot, cols_ref[j], preferred_element_type=jnp.float32))
        for part in range(0, TILE, LANES):
            top = jnp.maximum(top, scores[:, part : part + LANES])
    return top


def row_peaks(top, scale_ref, surr):
    rows = scale_ref.shape[0]
    peaks = [
        jnp.max((top[s * rows : (s + 1) * rows] * scale_ref[:, s : s + 1]).T, axis=0, keepdims=True)
        for s in range(surr)
    ]
    return jnp.concatenate(peaks, axis=0)


def first_score_kernel(
    frames, last_freq, spec_ref, turn_ref, near_ref, cols_hbm, peak_ref, far_ref, rot_ref, scale_ref, sem
):
    copy = start_copy(cols_hbm.at[pl.ds(near_ref.shape[0], far_ref.shape[0])], far_ref, sem)
    rotate(frames, last_freq, spec_ref, turn_ref, rot_ref, scale_ref)
    rot = rot_ref[...]
    top = raise_top(jnp.zeros((rot.shape[0], LANES), jnp.float32), rot, near_ref)
    copy.wait()
    peak_ref[...] = row_peaks(raise_top(top, rot, far_ref), scale_ref, peak_ref.shape[0])


def second_score_kernel(
    frames, last_freq, spec_ref, turn_ref, near_ref, far_ref, first_ref, own_ref, best_ref,
    rot_ref, scale_ref,
):
    rotate(frames, last_freq, spec_ref, turn_ref, rot_ref, scale_ref)
    rot = rot_ref[...]
    top = raise_top(jnp.zeros((rot.shape[0], LANES), jnp.float32), rot, near_ref)
    peaks = row_peaks(raise_top(top, rot, far_ref), scale_ref, first_ref.shape[0])
    first = first_ref[...]
    lane = lax.axis_index("lane")
    own_ref[lane] = first
    own_ref[1 - lane] = peaks
    best = jnp.max(jnp.maximum(first, peaks), axis=1, keepdims=True)
    lane_of = lax.broadcasted_iota(jnp.int32, (1, 1, best_ref.shape[2]), 2)
    row = jnp.zeros(lane_of.shape, jnp.float32)
    for s in range(best.shape[0]):
        row = jnp.where(lane_of == s, best[s : s + 1].reshape(1, 1, 1), row)
    best_ref[...] = jnp.broadcast_to(row, best_ref.shape)


def tm_exchange(value, n_tm):
    if n_tm == 2:
        other = lax.ppermute(value, "tm", [(0, 1), (1, 0)])
        first = lax.axis_index("tm") == 0
        return jnp.stack([jnp.where(first, value, other), jnp.where(first, other, value)])
    return lax.all_gather(value, "tm")


def lane_groups(n_grp, n_lane, n_tm):
    index = np.arange(n_grp * n_lane * n_tm).reshape(n_grp, n_lane, n_tm)
    return [index[:: 1 - 2 * lane, lane].T.reshape(-1).tolist() for lane in range(n_lane)]


def in_hbm(array):
    return pltpu.with_memory_space_constraint(array, pltpu.HBM)


def body(dims, series, slab_series, phase_index):
    n_grp, n_lane, n_tm = dims
    frames, columns = series.shape
    share, verts = slab_series.shape
    surr = phase_index.shape[0]
    freqs = phase_index.shape[1] * n_tm
    row_share = verts // n_tm
    rows = n_grp * row_share
    share_pad = round_up(phase_lane(share) + phase_chunks(freqs // n_tm, rows) * surr, LANES)
    half_pad = round_up(frames // 2, LANES)
    order = Order(freqs)
    last_freq = int(np.argmax(order.freq))
    points = 2 * order.pad
    limits = pltpu.CompilerParams(vmem_limit_bytes=24 * 2**20)

    codes = pl.pallas_call(
        functools.partial(encode_kernel, share, rows),
        out_shape=pltpu.VMEM((n_tm, n_grp, row_share, share_pad), jnp.int16),
        in_specs=[VMEM] * 2,
        out_specs=VMEM,
        compiler_params=limits,
    )(in_hbm(slab_series.T), in_hbm(phase_index))
    codes = codes.reshape(n_tm * n_grp, row_share, share_pad)
    received = lax.all_to_all(
        codes, ("grp", "lane", "tm"), 0, 0, tiled=True,
        axis_index_groups=lane_groups(n_grp, n_lane, n_tm),
    )

    n_tiles = columns // TILE
    col_high, col_low = column_tables(frames, order)
    cols = pl.pallas_call(
        column_kernel,
        out_shape=pltpu.HBM((n_tiles, points, TILE), jnp.bfloat16),
        in_specs=[HBM] * 3,
        out_specs=HBM,
        scratch_shapes=[
            pltpu.VMEM((n_tiles, frames, TILE), jnp.bfloat16),
            pltpu.VMEM(col_high.shape, jnp.bfloat16),
            pltpu.VMEM(col_low.shape, FLOAT8),
            pltpu.VMEM((n_tiles, points, TILE), jnp.bfloat16),
        ]
        + [pltpu.VMEM((2, half_pad, TILE), jnp.bfloat16)] * 2
        + [pltpu.VMEM((2, 2 * half_pad, TILE), FLOAT8)] * 2
        + [pltpu.SemaphoreType.DMA((n_tiles + 2,)), pltpu.SemaphoreType.DMA((n_tiles,))],
        compiler_params=limits,
        cost_estimate=pl.CostEstimate(
            flops=6 * order.pad * frames * columns, transcendentals=0, bytes_accessed=0
        ),
    )(in_hbm(series), in_hbm(col_high), in_hbm(col_low))

    received, cols = lax.optimization_barrier((received, cols))
    high, low, shift = slab_tables(frames, share, share_pad, n_tm, order)
    place = placement(order, freqs, n_tm, rows)
    n_near = n_tiles // 2
    rot_shape = pltpu.VMEM((surr * rows, points), jnp.bfloat16)
    spec, turn, near = pl.pallas_call(
        functools.partial(spectrum_kernel, share, frames, last_freq, freqs // n_tm),
        out_shape=(
            jax.ShapeDtypeStruct((rows, points), jnp.float32),
            jax.ShapeDtypeStruct((2 * surr, order.pad), jnp.float32),
            pltpu.VMEM((n_near, points, TILE), jnp.bfloat16),
        ),
        in_specs=[VMEM] + [HBM] * 4 + [VMEM],
        out_specs=(VMEM,) * 3,
        scratch_shapes=[
            pltpu.VMEM(high.shape, jnp.bfloat16),
            pltpu.VMEM(low.shape, FLOAT8),
            pltpu.VMEM(place.shape, FLOAT8),
            pltpu.SemaphoreType.DMA((6,)),
        ],
        compiler_params=limits,
        cost_estimate=pl.CostEstimate(
            flops=4 * points * n_tm * share_pad * rows, transcendentals=0, bytes_accessed=0
        ),
    )(
        received.reshape(n_tm, rows, share_pad),
        in_hbm(high), in_hbm(low), in_hbm(place), in_hbm(cols), shift,
    )
    other = lax.ppermute(spec, "lane", [(i, (i + 1) % n_lane) for i in range(n_lane)])
    score_cost = pl.CostEstimate(
        flops=2 * points * surr * rows * columns, transcendentals=0, bytes_accessed=0
    )
    first, far = pl.pallas_call(
        functools.partial(first_score_kernel, frames, last_freq),
        out_shape=(
            jax.ShapeDtypeStruct((surr, rows), jnp.float32),
            pltpu.VMEM((n_tiles - n_near, points, TILE), jnp.bfloat16),
        ),
        in_specs=[VMEM] * 3 + [HBM],
        out_specs=(VMEM, VMEM),
        scratch_shapes=[rot_shape, pltpu.VMEM((rows, surr), jnp.float32), pltpu.SemaphoreType.DMA],
        compiler_params=limits,
        cost_estimate=score_cost,
    )(spec, turn, near, in_hbm(cols))
    n_dev = n_grp * n_lane * n_tm
    own, best = pl.pallas_call(
        functools.partial(second_score_kernel, frames, last_freq),
        out_shape=(
            jax.ShapeDtypeStruct((2, surr, rows), jnp.float32),
            jax.ShapeDtypeStruct((n_dev, 1, LANES), jnp.float32),
        ),
        in_specs=[VMEM] * 5,
        out_specs=(VMEM, VMEM),
        scratch_shapes=[rot_shape, pltpu.VMEM((rows, surr), jnp.float32)],
        compiler_params=limits,
        cost_estimate=score_cost,
    )(other, turn, near, far, first)
    every = lax.all_to_all(best, ("grp", "lane", "tm"), 0, 0, tiled=True)
    peak_all = jnp.max(every, axis=(0, 1))[:surr]

    both = tm_exchange(own[:n_lane], n_tm).reshape(n_tm, n_lane, surr, n_grp, row_share)
    both = jnp.concatenate([both[:, :1], both[:, 1:, :, ::-1]], axis=1)
    tile_peak = jnp.transpose(both, (2, 3, 1, 0, 4)).reshape(surr, -1, 1)
    return tile_peak, peak_all


def solution(mesh):
    n_col, n_tm = mesh.shape["col"], mesh.shape["tm"]
    n_lane = 2 if n_col % 2 == 0 else 1
    dims = (n_col // n_lane, n_lane, n_tm)
    split = Mesh(mesh.devices.reshape(dims), ("grp", "lane", "tm"))
    col = ("grp", "lane")
    return jax.shard_map(
        functools.partial(body, dims),
        mesh=split,
        in_specs=(P(None, col), P("tm", col), P(None, "tm")),
        out_specs=(P(None, None, col), P()),
        check_vma=False,
    )
```

```python
import functools
import math

import jax
import jax.numpy as jnp
import ml_dtypes
import numpy as np
from jax import lax
from jax.experimental import pallas as pl
from jax.experimental.pallas import tpu as pltpu
from jax.sharding import Mesh, PartitionSpec as P

EPSILON = 1e-06
LANES = 128
CODE_TOP = 32767.0
LOW_SCALE = 2.0**14
COARSE_SCALE = 2.0**6
CODE_SCALE = COARSE_SCALE / LOW_SCALE
COL_SCALE = 2.0**8
FLOAT8 = jnp.float8_e4m3fn
VMEM = pl.BlockSpec(memory_space=pltpu.VMEM)
HBM = pl.BlockSpec(memory_space=pltpu.HBM)
TILE = 2 * LANES


def round_up(value, unit):
    return -(-value // unit) * unit


def split_table(table, axis, low_scale, coarse_scale):
    high = table.astype(ml_dtypes.bfloat16)
    low = (table - high.astype(np.float64)) * low_scale
    low = np.concatenate([low, table * coarse_scale], axis=axis).astype(ml_dtypes.float8_e4m3fn)
    return jnp.asarray(np.ascontiguousarray(high)), jnp.asarray(np.ascontiguousarray(low))


class Order:
    def __init__(self, freqs):
        self.half = round_up(-(-freqs // 2), 16)
        self.pad = round_up(2 * self.half, LANES)
        self.freq = np.zeros(self.pad, np.int64)
        self.freq[: freqs // 2] = np.arange(2, freqs + 1, 2)
        self.freq[self.half : self.half + freqs - freqs // 2] = np.arange(1, freqs + 1, 2)
        self.used = self.freq > 0

    def wave(self, points, frames):
        angles = (self.freq[:, None] * points[None, :] % frames) * (2.0 * math.pi / frames)
        return np.stack([np.cos(angles), np.sin(angles)]) * self.used[:, None]


def pad_last(array, size):
    return np.pad(array, [(0, 0)] * (array.ndim - 1) + [(0, size - array.shape[-1])])


def column_tables(frames, order):
    half_pad = round_up(frames // 2, LANES)
    wave = pad_last(order.wave(np.arange(frames // 2), frames), half_pad)[:, : 2 * order.half]
    wave = wave.reshape(2, 2, order.half, half_pad).transpose(1, 0, 2, 3)
    return split_table(wave.reshape(2, 2 * order.half, half_pad) * COL_SCALE, 2, 1.0, 1.0)


def slab_tables(frames, share, share_pad, n_tm, order):
    wave = pad_last(order.wave(np.arange(share), frames), share_pad).transpose(0, 2, 1)
    high, low = split_table(wave, 1, LOW_SCALE, COARSE_SCALE)
    sums = np.concatenate([wave[0].sum(axis=0), wave[1].sum(axis=0)])
    shift = order.wave(np.arange(n_tm) * share, frames).transpose(0, 2, 1)
    shift = np.concatenate([shift, shift], axis=2).reshape(2 * n_tm, 2 * order.pad)
    return high, low, jnp.asarray(np.concatenate([sums[None], shift]), jnp.float32)


def placement(order, freqs, n_tm, rows):
    share = freqs // n_tm
    share_pad = round_up(share, rows)
    index = order.freq - 1
    row = index // share * share_pad + index % share
    table = np.zeros((n_tm * share_pad, order.pad), ml_dtypes.float8_e4m3fn)
    table[row[order.used], np.nonzero(order.used)[0]] = 1.0
    return jnp.asarray(table)


def split_digits(value):
    scaled = value * 16.0
    first = scaled.astype(jnp.int32)
    rest = (scaled - first.astype(jnp.float32)) * 32768.0
    second = rest.astype(jnp.int32)
    third = ((rest - second.astype(jnp.float32)) * 32768.0).astype(jnp.int32)
    return first, second, third


def join_digits(first, second, third):
    return (
        first.astype(jnp.float32) * 2.0**-4
        + second.astype(jnp.float32) * 2.0**-19
        + third.astype(jnp.float32) * 2.0**-34
    )


def phase_lane(share):
    return round_up(share + 6, 8)


def phase_chunks(freq_share, rows):
    return -(-freq_share // rows)


def encode_kernel(share, rows, slab_ref, phase_ref, code_ref):
    values = slab_ref[...]
    verts = values.shape[0]
    n_tm, n_grp, row_share, share_pad = code_ref.shape
    highest = jnp.max(values, axis=1, keepdims=True)
    lowest = jnp.min(values, axis=1, keepdims=True)
    middle_digits = split_digits((highest + lowest) * 0.5)
    middle = join_digits(*middle_digits)
    offset = values - middle
    top_digits = split_digits(jnp.maximum(highest - middle, middle - lowest))
    step = join_digits(*top_digits) * (1.0 / CODE_TOP)
    inverse = jnp.where(step > 0.0, 1.0 / jnp.where(step > 0.0, step, 1.0), 0.0)
    codes = jnp.clip(jnp.round(offset * inverse), -CODE_TOP, CODE_TOP).astype(jnp.int32)
    codes = jnp.concatenate(
        [codes, jnp.zeros((verts, share_pad - share), jnp.int32)], axis=1
    )
    edge = share_pad - LANES
    tail = codes[:, edge:]
    lane = lax.broadcasted_iota(jnp.int32, (verts, LANES), 1) + (edge - share)
    for place, digit in enumerate(top_digits + middle_digits):
        tail = jnp.where(lane == place, digit, tail)

    surr, freq_share = phase_ref.shape
    chunks = phase_chunks(freq_share, rows)
    phase = phase_ref[...].astype(jnp.float32)
    phase = jnp.concatenate(
        [phase, jnp.zeros((surr, chunks * rows - freq_share), jnp.float32)], axis=1
    )
    phase = jnp.concatenate([phase[:, c * rows : (c + 1) * rows] for c in range(chunks)], axis=0)
    above = phase_lane(share) % LANES
    phase = jnp.concatenate(
        [
            jnp.zeros((above, rows), jnp.float32),
            phase,
            jnp.zeros((LANES - above - chunks * surr, rows), jnp.float32),
        ],
        axis=0,
    )
    group = lax.axis_index("grp")
    place = jnp.where(lax.axis_index("lane") == 0, group, n_grp - 1 - group)
    phase = pltpu.roll(phase, rows - place * row_share, 1).T[:row_share]
    phase = jnp.concatenate([phase.astype(jnp.int32)] * n_tm, axis=0)
    codes = jnp.concatenate([codes[:, :edge], tail + phase], axis=1)
    for m in range(n_tm):
        block = codes[m * row_share : (m + 1) * row_share].astype(jnp.int16)
        for g in range(n_grp):
            code_ref[m, g] = block


def start_copy(source, target, sem):
    copy = pltpu.make_async_copy(source, target, sem)
    copy.start()
    return copy


def wait_all(copies):
    for copy in copies:
        copy.wait()


def column_kernel(
    series_hbm, high_hbm, low_hbm, out_hbm,
    series, high, low, out, normed_0, normed_1, coarse_0, coarse_1, load_sems, store_sems,
):
    n_tiles, frames, _ = series.shape
    half = frames // 2
    half_pad = high.shape[2]
    freq_half = high.shape[1] // 2
    freq_pad = out.shape[1] // 2
    gap = freq_pad - 2 * freq_half
    normed_refs, coarse_refs = (normed_0, normed_1), (coarse_0, coarse_1)

    def load_tile(j):
        return start_copy(series_hbm.at[:, pl.ds(j * TILE, TILE)], series.at[j], load_sems.at[j])

    tile_copies = [load_tile(0)]
    table_copies = [
        start_copy(high_hbm, high, load_sems.at[n_tiles]),
        start_copy(low_hbm, low, load_sems.at[n_tiles + 1]),
    ]
    tile_copies += [load_tile(j) for j in range(1, n_tiles)]

    def normalize(j):
        normed_ref, coarse_ref = normed_refs[j % 2], coarse_refs[j % 2]
        values = series[j].astype(jnp.float32)
        centered = values - jnp.sum(values, axis=0, keepdims=True) * (1.0 / frames)
        total = jnp.sum(centered * centered, axis=0, keepdims=True)
        normed = centered * (lax.rsqrt(total + EPSILON) * COL_SCALE)
        first, second = (
            jnp.concatenate([part, jnp.zeros((half_pad - half, TILE), jnp.float32)], axis=0).astype(
                jnp.bfloat16
            )
            for part in (normed[:half], normed[half:])
        )
        for parity, other in enumerate((second, -second)):
            rounded = first + other
            added = rounded - first
            rest = (first - (rounded - added)) + (other - added)
            normed_ref[parity] = rounded
            coarse_ref[parity, pl.ds(0, half_pad), :] = rounded.astype(FLOAT8)
            coarse_ref[parity, pl.ds(half_pad, half_pad), :] = rest.astype(FLOAT8)

    tile_copies[0].wait()
    normalize(0)
    wait_all(table_copies + tile_copies[1:2])
    stores = []
    for j in range(n_tiles):
        if j == 1:
            wait_all(tile_copies[2:])
        if j + 1 < n_tiles:
            normalize(j + 1)
        for parity in range(2):
            sums = jnp.dot(
                high[parity], normed_refs[j % 2][parity], preferred_element_type=jnp.float32
            )
            rest = jnp.dot(
                low[parity], coarse_refs[j % 2][parity], preferred_element_type=jnp.float32
            )
            sums = (sums + rest).astype(jnp.bfloat16)
            for q in range(2):
                span = pl.ds(q * freq_pad + parity * freq_half, freq_half)
                out[j, span, :] = sums[q * freq_half : (q + 1) * freq_half]
        for q in range(2):
            if gap:
                span = pl.ds(q * freq_pad + 2 * freq_half, gap)
                out[j, span, :] = jnp.zeros((gap, TILE), jnp.bfloat16)
        stores.append(start_copy(out.at[j], out_hbm.at[j], store_sems.at[j]))
    wait_all(stores)


def surrogate_turns(frames, last_freq, phases, place_ref):
    surr = phases[0].shape[0]
    freq_pad = place_ref.shape[1]
    digits = []
    for phase in phases:
        parts = [phase >> 8, (phase >> 4) & 15, phase & 15]
        digits.append(jnp.concatenate(parts, axis=0).astype(jnp.float32))
    digits = jnp.concatenate(digits, axis=1).astype(FLOAT8)
    placed = jnp.dot(digits, place_ref[...], preferred_element_type=jnp.float32)
    turn = placed[:surr] * 256.0 + placed[surr : 2 * surr] * 16.0 + placed[2 * surr :]
    freq = lax.broadcasted_iota(jnp.int32, (1, freq_pad), 1)
    weight = jnp.where(freq == last_freq, 1.0 / frames, 2.0 / frames)
    cos, sin = turn_waves(frames, turn)
    return cos * weight, sin * weight


def turn_waves(frames, turn):
    quarter = frames / 4
    quadrant = jnp.floor(turn * (1.0 / quarter) + 0.5)
    x = (turn - quadrant * quarter) * (2.0 * math.pi / frames)
    y = x * x
    cos = 1.0 + y * (-1 / 2 + y * (1 / 24 + y * (-1 / 720 + y * (1 / 40320 - y * (1 / 3628800)))))
    sin = x * (1.0 + y * (-1 / 6 + y * (1 / 120 + y * (-1 / 5040 + y * (1 / 362880)))))
    odd = (quadrant == 1.0) | (quadrant == 3.0)
    left = (quadrant == 1.0) | (quadrant == 2.0)
    down = (quadrant == 2.0) | (quadrant == 3.0)
    near = jnp.where(odd, sin, cos)
    far = jnp.where(odd, cos, sin)
    return jnp.where(left, -near, near), jnp.where(down, -far, far)


def rotate(frames, last_freq, spec_ref, turn_ref, rot_ref, scale_ref):
    rows = spec_ref.shape[0]
    surr, freq_pad = turn_ref.shape[0] // 2, turn_ref.shape[1]
    spec_cos = spec_ref[:, :freq_pad]
    spec_sin = spec_ref[:, freq_pad:]
    freq = lax.broadcasted_iota(jnp.int32, (1, freq_pad), 1)
    pair = jnp.where(freq != last_freq, (2.0 / frames) ** 2 * (frames / 2.0), 0.0)
    common = jnp.sum((spec_cos * spec_cos + spec_sin * spec_sin) * pair, axis=1, keepdims=True)
    block = last_freq // LANES * LANES
    last = jnp.where(freq[:, block : block + LANES] == last_freq, float(frames), 0.0)
    for s in range(surr):
        cos_row = turn_ref[pl.ds(s, 1), :]
        sin_row = turn_ref[pl.ds(surr + s, 1), :]
        rot_real = spec_cos * cos_row + spec_sin * sin_row
        rot_imag = spec_cos * sin_row - spec_sin * cos_row
        at_last = rot_real[:, block : block + LANES]
        energy = common + jnp.sum(at_last * at_last * last, axis=1, keepdims=True)
        scale_ref[:, s : s + 1] = lax.rsqrt(energy + EPSILON) * (math.sqrt(frames) / COL_SCALE**2)
        span = pl.ds(s * rows, rows)
        rot_ref[span, :freq_pad] = rot_real.astype(jnp.bfloat16)
        rot_ref[span, freq_pad:] = (-rot_imag).astype(jnp.bfloat16)


def spectrum_kernel(
    share, frames, last_freq, freq_share,
    codes_ref, high_hbm, low_hbm, place_hbm, cols_hbm, shift_ref,
    spec_ref, turn_ref, cols_ref,
    high, low, place, sems,
):
    n_tm, rows, share_pad = codes_ref.shape
    freq_pad = high.shape[2]
    place_copy = start_copy(place_hbm, place, sems.at[4])
    copies = [
        [
            start_copy(high_hbm.at[q], high.at[q], sems.at[2 * q]),
            start_copy(low_hbm.at[q], low.at[q], sems.at[1 + 2 * q]),
        ]
        for q in range(2)
    ]
    cols_copy = start_copy(cols_hbm.at[pl.ds(0, cols_ref.shape[0])], cols_ref, sems.at[5])
    codes = codes_ref[...].reshape(n_tm * rows, share_pad).astype(jnp.int32)
    upper = ((codes + 128) >> 8) << 8
    lower = (codes - upper).astype(jnp.float32)
    upper = upper.astype(jnp.float32)
    coarse = jnp.concatenate([upper * CODE_SCALE, lower], axis=1).astype(FLOAT8)
    upper = upper.astype(jnp.bfloat16)
    digits = [codes[:, share + p : share + p + 1] for p in range(6)]
    step = join_digits(*digits[:3]) * (1.0 / CODE_TOP)
    middle = join_digits(*digits[3:])
    surr = turn_ref.shape[0] // 2
    chunks = phase_chunks(freq_share, rows)
    above = phase_lane(share) % LANES
    phases = []
    for m in range(n_tm):
        block = codes[m * rows : (m + 1) * rows, share_pad - LANES :].astype(jnp.float32).T
        block = block[above : above + round_up(chunks * surr, 8)].astype(jnp.int32)
        parts = [block[c * surr : (c + 1) * surr] for c in range(chunks)]
        phases.append(jnp.concatenate(parts, axis=1))
    place_copy.wait()
    turn_cos, turn_sin = surrogate_turns(frames, last_freq, phases, place)
    parts = []
    for q in range(2):
        wait_all(copies[q])
        part = jnp.dot(upper, high[q], preferred_element_type=jnp.float32)
        part += jnp.dot(coarse, low[q], preferred_element_type=jnp.float32) * (1.0 / COARSE_SCALE)
        part = part * step + middle * shift_ref[0:1, q * freq_pad : (q + 1) * freq_pad]
        if n_tm == 2:
            sign = shift_ref[2:3, :freq_pad]
            spec_ref[:, q * freq_pad : (q + 1) * freq_pad] = part[:rows] + part[rows:] * sign
        parts.append(part)
    if n_tm != 2:
        spec_cos = jnp.zeros((rows, freq_pad), jnp.float32)
        spec_sin = jnp.zeros((rows, freq_pad), jnp.float32)
        for m in range(n_tm):
            part_cos, part_sin = (part[m * rows : (m + 1) * rows] for part in parts)
            shift_cos = shift_ref[1 + m : 2 + m, :freq_pad]
            shift_sin = shift_ref[1 + n_tm + m : 2 + n_tm + m, :freq_pad]
            spec_cos += part_cos * shift_cos - part_sin * shift_sin
            spec_sin += part_sin * shift_cos + part_cos * shift_sin
        spec_ref[:, :freq_pad] = spec_cos
        spec_ref[:, freq_pad:] = spec_sin
    turn_ref[pl.ds(0, surr), :] = turn_cos
    turn_ref[pl.ds(surr, surr), :] = turn_sin
    cols_copy.wait()


def raise_top(top, rot, cols_ref):
    for j in range(cols_ref.shape[0]):
        scores = jnp.abs(jnp.dot(rot, cols_ref[j], preferred_element_type=jnp.float32))
        for part in range(0, TILE, LANES):
            top = jnp.maximum(top, scores[:, part : part + LANES])
    return top


def row_peaks(top, scale_ref, surr):
    rows = scale_ref.shape[0]
    peaks = [
        jnp.max((top[s * rows : (s + 1) * rows] * scale_ref[:, s : s + 1]).T, axis=0, keepdims=True)
        for s in range(surr)
    ]
    return jnp.concatenate(peaks, axis=0)


def first_score_kernel(
    frames, last_freq, spec_ref, turn_ref, near_ref, cols_hbm, peak_ref, far_ref, rot_ref, scale_ref, sem
):
    copy = start_copy(cols_hbm.at[pl.ds(near_ref.shape[0], far_ref.shape[0])], far_ref, sem)
    rotate(frames, last_freq, spec_ref, turn_ref, rot_ref, scale_ref)
    rot = rot_ref[...]
    top = raise_top(jnp.zeros((rot.shape[0], LANES), jnp.float32), rot, near_ref)
    copy.wait()
    peak_ref[...] = row_peaks(raise_top(top, rot, far_ref), scale_ref, peak_ref.shape[0])


def second_score_kernel(
    frames, last_freq, spec_ref, turn_ref, near_ref, far_ref, first_ref, own_ref, best_ref,
    rot_ref, scale_ref,
):
    rotate(frames, last_freq, spec_ref, turn_ref, rot_ref, scale_ref)
    rot = rot_ref[...]
    top = raise_top(jnp.zeros((rot.shape[0], LANES), jnp.float32), rot, near_ref)
    peaks = row_peaks(raise_top(top, rot, far_ref), scale_ref, first_ref.shape[0])
    first = first_ref[...]
    lane = lax.axis_index("lane")
    own_ref[lane] = first
    own_ref[1 - lane] = peaks
    best = jnp.max(jnp.maximum(first, peaks), axis=1, keepdims=True)
    lane_of = lax.broadcasted_iota(jnp.int32, (1, 1, best_ref.shape[2]), 2)
    row = jnp.zeros(lane_of.shape, jnp.float32)
    for s in range(best.shape[0]):
        row = jnp.where(lane_of == s, best[s : s + 1].reshape(1, 1, 1), row)
    best_ref[...] = jnp.broadcast_to(row, best_ref.shape)


def tm_exchange(value, n_tm):
    if n_tm == 2:
        other = lax.ppermute(value, "tm", [(0, 1), (1, 0)])
        first = lax.axis_index("tm") == 0
        return jnp.stack([jnp.where(first, value, other), jnp.where(first, other, value)])
    return lax.all_gather(value, "tm")


def lane_groups(n_grp, n_lane, n_tm):
    index = np.arange(n_grp * n_lane * n_tm).reshape(n_grp, n_lane, n_tm)
    return [index[:: 1 - 2 * lane, lane].T.reshape(-1).tolist() for lane in range(n_lane)]


def in_hbm(array):
    return pltpu.with_memory_space_constraint(array, pltpu.HBM)


def body(dims, series, slab_series, phase_index):
    n_grp, n_lane, n_tm = dims
    frames, columns = series.shape
    share, verts = slab_series.shape
    surr = phase_index.shape[0]
    freqs = phase_index.shape[1] * n_tm
    row_share = verts // n_tm
    rows = n_grp * row_share
    share_pad = round_up(phase_lane(share) + phase_chunks(freqs // n_tm, rows) * surr, LANES)
    half_pad = round_up(frames // 2, LANES)
    order = Order(freqs)
    last_freq = int(np.argmax(order.freq))
    points = 2 * order.pad
    limits = pltpu.CompilerParams(vmem_limit_bytes=24 * 2**20)

    codes = pl.pallas_call(
        functools.partial(encode_kernel, share, rows),
        out_shape=pltpu.VMEM((n_tm, n_grp, row_share, share_pad), jnp.int16),
        in_specs=[VMEM] * 2,
        out_specs=VMEM,
        compiler_params=limits,
    )(in_hbm(slab_series.T), in_hbm(phase_index))
    codes = codes.reshape(n_tm * n_grp, row_share, share_pad)
    received = lax.all_to_all(
        codes, ("grp", "lane", "tm"), 0, 0, tiled=True,
        axis_index_groups=lane_groups(n_grp, n_lane, n_tm),
    )

    n_tiles = columns // TILE
    col_high, col_low = column_tables(frames, order)
    cols = pl.pallas_call(
        column_kernel,
        out_shape=pltpu.HBM((n_tiles, points, TILE), jnp.bfloat16),
        in_specs=[HBM] * 3,
        out_specs=HBM,
        scratch_shapes=[
            pltpu.VMEM((n_tiles, frames, TILE), jnp.bfloat16),
            pltpu.VMEM(col_high.shape, jnp.bfloat16),
            pltpu.VMEM(col_low.shape, FLOAT8),
            pltpu.VMEM((n_tiles, points, TILE), jnp.bfloat16),
        ]
        + [pltpu.VMEM((2, half_pad, TILE), jnp.bfloat16)] * 2
        + [pltpu.VMEM((2, 2 * half_pad, TILE), FLOAT8)] * 2
        + [pltpu.SemaphoreType.DMA((n_tiles + 2,)), pltpu.SemaphoreType.DMA((n_tiles,))],
        compiler_params=limits,
        cost_estimate=pl.CostEstimate(
            flops=6 * order.pad * frames * columns, transcendentals=0, bytes_accessed=0
        ),
    )(in_hbm(series), in_hbm(col_high), in_hbm(col_low))

    received, cols = lax.optimization_barrier((received, cols))
    high, low, shift = slab_tables(frames, share, share_pad, n_tm, order)
    place = placement(order, freqs, n_tm, rows)
    n_near = n_tiles // 2
    rot_shape = pltpu.VMEM((surr * rows, points), jnp.bfloat16)
    spec, turn, near = pl.pallas_call(
        functools.partial(spectrum_kernel, share, frames, last_freq, freqs // n_tm),
        out_shape=(
            jax.ShapeDtypeStruct((rows, points), jnp.float32),
            jax.ShapeDtypeStruct((2 * surr, order.pad), jnp.float32),
            pltpu.VMEM((n_near, points, TILE), jnp.bfloat16),
        ),
        in_specs=[VMEM] + [HBM] * 4 + [VMEM],
        out_specs=(VMEM,) * 3,
        scratch_shapes=[
            pltpu.VMEM(high.shape, jnp.bfloat16),
            pltpu.VMEM(low.shape, FLOAT8),
            pltpu.VMEM(place.shape, FLOAT8),
            pltpu.SemaphoreType.DMA((6,)),
        ],
        compiler_params=limits,
        cost_estimate=pl.CostEstimate(
            flops=4 * points * n_tm * share_pad * rows, transcendentals=0, bytes_accessed=0
        ),
    )(
        received.reshape(n_tm, rows, share_pad),
        in_hbm(high), in_hbm(low), in_hbm(place), in_hbm(cols), shift,
    )
    other = lax.ppermute(spec, "lane", [(i, (i + 1) % n_lane) for i in range(n_lane)])
    score_cost = pl.CostEstimate(
        flops=2 * points * surr * rows * columns, transcendentals=0, bytes_accessed=0
    )
    first, far = pl.pallas_call(
        functools.partial(first_score_kernel, frames, last_freq),
        out_shape=(
            jax.ShapeDtypeStruct((surr, rows), jnp.float32),
            pltpu.VMEM((n_tiles - n_near, points, TILE), jnp.bfloat16),
        ),
        in_specs=[VMEM] * 3 + [HBM],
        out_specs=(VMEM, VMEM),
        scratch_shapes=[rot_shape, pltpu.VMEM((rows, surr), jnp.float32), pltpu.SemaphoreType.DMA],
        compiler_params=limits,
        cost_estimate=score_cost,
    )(spec, turn, near, in_hbm(cols))
    n_dev = n_grp * n_lane * n_tm
    own, best = pl.pallas_call(
        functools.partial(second_score_kernel, frames, last_freq),
        out_shape=(
            jax.ShapeDtypeStruct((2, surr, rows), jnp.float32),
            jax.ShapeDtypeStruct((n_dev, 1, LANES), jnp.float32),
        ),
        in_specs=[VMEM] * 5,
        out_specs=(VMEM, VMEM),
        scratch_shapes=[rot_shape, pltpu.VMEM((rows, surr), jnp.float32)],
        compiler_params=limits,
        cost_estimate=score_cost,
    )(other, turn, near, far, first)
    every = lax.all_to_all(best, ("grp", "lane", "tm"), 0, 0, tiled=True)
    peak_all = jnp.max(every, axis=(0, 1))[:surr]

    both = tm_exchange(own[:n_lane], n_tm).reshape(n_tm, n_lane, surr, n_grp, row_share)
    both = jnp.concatenate([both[:, :1], both[:, 1:, :, ::-1]], axis=1)
    tile_peak = jnp.transpose(both, (2, 3, 1, 0, 4)).reshape(surr, -1, 1)
    return tile_peak, peak_all


def solution(mesh):
    n_col, n_tm = mesh.shape["col"], mesh.shape["tm"]
    n_lane = 2 if n_col % 2 == 0 else 1
    dims = (n_col // n_lane, n_lane, n_tm)
    split = Mesh(mesh.devices.reshape(dims), ("grp", "lane", "tm"))
    col = ("grp", "lane")
    return jax.shard_map(
        functools.partial(body, dims),
        mesh=split,
        in_specs=(P(None, col), P("tm", col), P(None, "tm")),
        out_specs=(P(None, None, col), P()),
        check_vma=False,
    )
```

```python
import functools
import math

import jax
import jax.numpy as jnp
import ml_dtypes
import numpy as np
from jax import lax
from jax.experimental import pallas as pl
from jax.experimental.pallas import tpu as pltpu
from jax.sharding import Mesh, PartitionSpec as P

EPSILON = 1e-06
LANES = 128
CODE_TOP = 32767.0
LOW_SCALE = 2.0**14
COARSE_SCALE = 2.0**6
CODE_SCALE = COARSE_SCALE / LOW_SCALE
COL_SCALE = 2.0**8
FLOAT8 = jnp.float8_e4m3fn
VMEM = pl.BlockSpec(memory_space=pltpu.VMEM)
HBM = pl.BlockSpec(memory_space=pltpu.HBM)
TILE = 2 * LANES


def round_up(value, unit):
    return -(-value // unit) * unit


def split_table(table, axis, low_scale, coarse_scale):
    high = table.astype(ml_dtypes.bfloat16)
    low = (table - high.astype(np.float64)) * low_scale
    low = np.concatenate([low, table * coarse_scale], axis=axis).astype(ml_dtypes.float8_e4m3fn)
    return jnp.asarray(np.ascontiguousarray(high)), jnp.asarray(np.ascontiguousarray(low))


class Order:
    def __init__(self, freqs):
        self.half = round_up(-(-freqs // 2), 16)
        self.pad = round_up(2 * self.half, LANES)
        self.freq = np.zeros(self.pad, np.int64)
        self.freq[: freqs // 2] = np.arange(2, freqs + 1, 2)
        self.freq[self.half : self.half + freqs - freqs // 2] = np.arange(1, freqs + 1, 2)
        self.used = self.freq > 0

    def wave(self, points, frames):
        angles = (self.freq[:, None] * points[None, :] % frames) * (2.0 * math.pi / frames)
        return np.stack([np.cos(angles), np.sin(angles)]) * self.used[:, None]


def pad_last(array, size):
    return np.pad(array, [(0, 0)] * (array.ndim - 1) + [(0, size - array.shape[-1])])


def column_tables(frames, order):
    half_pad = round_up(frames // 2, LANES)
    wave = pad_last(order.wave(np.arange(frames // 2), frames), half_pad)[:, : 2 * order.half]
    wave = wave.reshape(2, 2, order.half, half_pad).transpose(1, 0, 2, 3)
    return split_table(wave.reshape(2, 2 * order.half, half_pad) * COL_SCALE, 2, 1.0, 1.0)


def slab_tables(frames, share, share_pad, n_tm, order):
    wave = pad_last(order.wave(np.arange(share), frames), share_pad).transpose(0, 2, 1)
    high, low = split_table(wave, 1, LOW_SCALE, COARSE_SCALE)
    sums = np.concatenate([wave[0].sum(axis=0), wave[1].sum(axis=0)])
    shift = order.wave(np.arange(n_tm) * share, frames).transpose(0, 2, 1)
    shift = np.concatenate([shift, shift], axis=2).reshape(2 * n_tm, 2 * order.pad)
    return high, low, jnp.asarray(np.concatenate([sums[None], shift]), jnp.float32)


def placement(order, freqs, n_tm, rows):
    share = freqs // n_tm
    share_pad = round_up(share, rows)
    index = order.freq - 1
    row = index // share * share_pad + index % share
    table = np.zeros((n_tm * share_pad, order.pad), ml_dtypes.float8_e4m3fn)
    table[row[order.used], np.nonzero(order.used)[0]] = 1.0
    return jnp.asarray(table)


def split_digits(value):
    scaled = value * 16.0
    first = scaled.astype(jnp.int32)
    rest = (scaled - first.astype(jnp.float32)) * 32768.0
    second = rest.astype(jnp.int32)
    third = ((rest - second.astype(jnp.float32)) * 32768.0).astype(jnp.int32)
    return first, second, third


def join_digits(first, second, third):
    return (
        first.astype(jnp.float32) * 2.0**-4
        + second.astype(jnp.float32) * 2.0**-19
        + third.astype(jnp.float32) * 2.0**-34
    )


def phase_lane(share):
    return round_up(share + 6, 8)


def phase_chunks(freq_share, rows):
    return -(-freq_share // rows)


def encode_kernel(share, rows, slab_ref, phase_ref, code_ref):
    values = slab_ref[...]
    verts = values.shape[0]
    n_tm, n_grp, row_share, share_pad = code_ref.shape
    highest = jnp.max(values, axis=1, keepdims=True)
    lowest = jnp.min(values, axis=1, keepdims=True)
    middle_digits = split_digits((highest + lowest) * 0.5)
    middle = join_digits(*middle_digits)
    offset = values - middle
    top_digits = split_digits(jnp.maximum(highest - middle, middle - lowest))
    step = join_digits(*top_digits) * (1.0 / CODE_TOP)
    inverse = jnp.where(step > 0.0, 1.0 / jnp.where(step > 0.0, step, 1.0), 0.0)
    codes = jnp.clip(jnp.round(offset * inverse), -CODE_TOP, CODE_TOP).astype(jnp.int32)
    codes = jnp.concatenate(
        [codes, jnp.zeros((verts, share_pad - share), jnp.int32)], axis=1
    )
    edge = share_pad - LANES
    tail = codes[:, edge:]
    lane = lax.broadcasted_iota(jnp.int32, (verts, LANES), 1) + (edge - share)
    for place, digit in enumerate(top_digits + middle_digits):
        tail = jnp.where(lane == place, digit, tail)

    surr, freq_share = phase_ref.shape
    chunks = phase_chunks(freq_share, rows)
    phase = phase_ref[...].astype(jnp.float32)
    phase = jnp.concatenate(
        [phase, jnp.zeros((surr, chunks * rows - freq_share), jnp.float32)], axis=1
    )
    phase = jnp.concatenate([phase[:, c * rows : (c + 1) * rows] for c in range(chunks)], axis=0)
    above = phase_lane(share) % LANES
    phase = jnp.concatenate(
        [
            jnp.zeros((above, rows), jnp.float32),
            phase,
            jnp.zeros((LANES - above - chunks * surr, rows), jnp.float32),
        ],
        axis=0,
    )
    group = lax.axis_index("grp")
    place = jnp.where(lax.axis_index("lane") == 0, group, n_grp - 1 - group)
    phase = pltpu.roll(phase, rows - place * row_share, 1).T[:row_share]
    phase = jnp.concatenate([phase.astype(jnp.int32)] * n_tm, axis=0)
    codes = jnp.concatenate([codes[:, :edge], tail + phase], axis=1)
    for m in range(n_tm):
        block = codes[m * row_share : (m + 1) * row_share].astype(jnp.int16)
        for g in range(n_grp):
            code_ref[m, g] = block


def start_copy(source, target, sem):
    copy = pltpu.make_async_copy(source, target, sem)
    copy.start()
    return copy


def wait_all(copies):
    for copy in copies:
        copy.wait()


def column_kernel(
    series_hbm, high_hbm, low_hbm, out_hbm,
    series, high, low, out, normed_0, normed_1, coarse_0, coarse_1, load_sems, store_sems,
):
    n_tiles, frames, _ = series.shape
    half = frames // 2
    half_pad = high.shape[2]
    freq_half = high.shape[1] // 2
    freq_pad = out.shape[1] // 2
    gap = freq_pad - 2 * freq_half
    normed_refs, coarse_refs = (normed_0, normed_1), (coarse_0, coarse_1)

    def load_tile(j):
        return start_copy(series_hbm.at[:, pl.ds(j * TILE, TILE)], series.at[j], load_sems.at[j])

    tile_copies = [load_tile(0)]
    table_copies = [
        start_copy(high_hbm, high, load_sems.at[n_tiles]),
        start_copy(low_hbm, low, load_sems.at[n_tiles + 1]),
    ]
    tile_copies += [load_tile(j) for j in range(1, n_tiles)]

    def normalize(j):
        normed_ref, coarse_ref = normed_refs[j % 2], coarse_refs[j % 2]
        values = series[j].astype(jnp.float32)
        centered = values - jnp.sum(values, axis=0, keepdims=True) * (1.0 / frames)
        total = jnp.sum(centered * centered, axis=0, keepdims=True)
        normed = centered * (lax.rsqrt(total + EPSILON) * COL_SCALE)
        first, second = (
            jnp.concatenate([part, jnp.zeros((half_pad - half, TILE), jnp.float32)], axis=0).astype(
                jnp.bfloat16
            )
            for part in (normed[:half], normed[half:])
        )
        for parity, other in enumerate((second, -second)):
            rounded = first + other
            added = rounded - first
            rest = (first - (rounded - added)) + (other - added)
            normed_ref[parity] = rounded
            coarse_ref[parity, pl.ds(0, half_pad), :] = rounded.astype(FLOAT8)
            coarse_ref[parity, pl.ds(half_pad, half_pad), :] = rest.astype(FLOAT8)

    tile_copies[0].wait()
    normalize(0)
    wait_all(table_copies + tile_copies[1:2])
    stores = []
    if gap:
        for q in range(2):
            span = pl.ds(q * freq_pad + 2 * freq_half, gap)
            out[:, span, :] = jnp.zeros((n_tiles, gap, TILE), jnp.bfloat16)
    for j in range(n_tiles):
        if j == 1:
            wait_all(tile_copies[2:])
        if j + 1 < n_tiles:
            normalize(j + 1)
        for parity in range(2):
            sums = jnp.dot(
                high[parity], normed_refs[j % 2][parity], preferred_element_type=jnp.float32
            )
            rest = jnp.dot(
                low[parity], coarse_refs[j % 2][parity], preferred_element_type=jnp.float32
            )
            sums = (sums + rest).astype(jnp.bfloat16)
            for q in range(2):
                span = pl.ds(q * freq_pad + parity * freq_half, freq_half)
                out[j, span, :] = sums[q * freq_half : (q + 1) * freq_half]
                if j + 1 == n_tiles:
                    start = q * freq_pad + parity * freq_half
                    part = pl.ds(start, freq_half + parity * gap)
                    place = n_tiles - 1 + 2 * parity + q
                    stores.append(start_copy(out.at[j, part], out_hbm.at[j, part], store_sems.at[place]))
        if j + 1 < n_tiles:
            stores.append(start_copy(out.at[j], out_hbm.at[j], store_sems.at[j]))
    wait_all(stores)


def surrogate_turns(frames, last_freq, phases, place_ref):
    surr = phases[0].shape[0]
    freq_pad = place_ref.shape[1]
    digits = []
    for phase in phases:
        parts = [phase >> 8, (phase >> 4) & 15, phase & 15]
        digits.append(jnp.concatenate(parts, axis=0).astype(jnp.float32))
    digits = jnp.concatenate(digits, axis=1).astype(FLOAT8)
    placed = jnp.dot(digits, place_ref[...], preferred_element_type=jnp.float32)
    turn = placed[:surr] * 256.0 + placed[surr : 2 * surr] * 16.0 + placed[2 * surr :]
    freq = lax.broadcasted_iota(jnp.int32, (1, freq_pad), 1)
    weight = jnp.where(freq == last_freq, 1.0 / frames, 2.0 / frames)
    cos, sin = turn_waves(frames, turn)
    return cos * weight, sin * weight


def turn_waves(frames, turn):
    quarter = frames / 4
    quadrant = jnp.floor(turn * (1.0 / quarter) + 0.5)
    x = (turn - quadrant * quarter) * (2.0 * math.pi / frames)
    y = x * x
    cos = 1.0 + y * (-1 / 2 + y * (1 / 24 + y * (-1 / 720 + y * (1 / 40320 - y * (1 / 3628800)))))
    sin = x * (1.0 + y * (-1 / 6 + y * (1 / 120 + y * (-1 / 5040 + y * (1 / 362880)))))
    odd = (quadrant == 1.0) | (quadrant == 3.0)
    left = (quadrant == 1.0) | (quadrant == 2.0)
    down = (quadrant == 2.0) | (quadrant == 3.0)
    near = jnp.where(odd, sin, cos)
    far = jnp.where(odd, cos, sin)
    return jnp.where(left, -near, near), jnp.where(down, -far, far)


def rotate(frames, last_freq, spec_ref, turn_ref, rot_ref, scale_ref):
    rows = spec_ref.shape[0]
    surr, freq_pad = turn_ref.shape[0] // 2, turn_ref.shape[1]
    spec_cos = spec_ref[:, :freq_pad]
    spec_sin = spec_ref[:, freq_pad:]
    freq = lax.broadcasted_iota(jnp.int32, (1, freq_pad), 1)
    pair = jnp.where(freq != last_freq, (2.0 / frames) ** 2 * (frames / 2.0), 0.0)
    common = jnp.sum((spec_cos * spec_cos + spec_sin * spec_sin) * pair, axis=1, keepdims=True)
    block = last_freq // LANES * LANES
    last = jnp.where(freq[:, block : block + LANES] == last_freq, float(frames), 0.0)
    for s in range(surr):
        cos_row = turn_ref[pl.ds(s, 1), :]
        sin_row = turn_ref[pl.ds(surr + s, 1), :]
        rot_real = spec_cos * cos_row + spec_sin * sin_row
        rot_imag = spec_cos * sin_row - spec_sin * cos_row
        at_last = rot_real[:, block : block + LANES]
        energy = common + jnp.sum(at_last * at_last * last, axis=1, keepdims=True)
        scale_ref[:, s : s + 1] = lax.rsqrt(energy + EPSILON) * (math.sqrt(frames) / COL_SCALE**2)
        span = pl.ds(s * rows, rows)
        rot_ref[span, :freq_pad] = rot_real.astype(jnp.bfloat16)
        rot_ref[span, freq_pad:] = (-rot_imag).astype(jnp.bfloat16)


def spectrum_kernel(
    share, frames, last_freq, freq_share,
    codes_ref, high_hbm, low_hbm, place_hbm, cols_hbm, shift_ref,
    spec_ref, turn_ref, cols_ref,
    high, low, place, sems,
):
    n_tm, rows, share_pad = codes_ref.shape
    freq_pad = high.shape[2]
    copies = [
        [
            start_copy(high_hbm.at[q], high.at[q], sems.at[2 * q]),
            start_copy(low_hbm.at[q], low.at[q], sems.at[1 + 2 * q]),
        ]
        for q in range(2)
    ]
    place_copy = start_copy(place_hbm, place, sems.at[4])
    cols_copy = start_copy(cols_hbm.at[pl.ds(0, cols_ref.shape[0])], cols_ref, sems.at[5])
    codes = codes_ref[...].reshape(n_tm * rows, share_pad).astype(jnp.int32)
    upper = ((codes + 128) >> 8) << 8
    lower = (codes - upper).astype(jnp.float32)
    upper = upper.astype(jnp.float32)
    coarse = jnp.concatenate([upper * CODE_SCALE, lower], axis=1).astype(FLOAT8)
    upper = upper.astype(jnp.bfloat16)
    digits = [codes[:, share + p : share + p + 1] for p in range(6)]
    step = join_digits(*digits[:3]) * (1.0 / CODE_TOP)
    middle = join_digits(*digits[3:])
    surr = turn_ref.shape[0] // 2
    chunks = phase_chunks(freq_share, rows)
    above = phase_lane(share) % LANES
    phases = []
    for m in range(n_tm):
        block = codes[m * rows : (m + 1) * rows, share_pad - LANES :].astype(jnp.float32).T
        block = block[above : above + round_up(chunks * surr, 8)].astype(jnp.int32)
        parts = [block[c * surr : (c + 1) * surr] for c in range(chunks)]
        phases.append(jnp.concatenate(parts, axis=1))
    parts = []
    for q in range(2):
        wait_all(copies[q] + [place_copy] * q)
        part = jnp.dot(upper, high[q], preferred_element_type=jnp.float32)
        part += jnp.dot(coarse, low[q], preferred_element_type=jnp.float32) * (1.0 / COARSE_SCALE)
        part = part * step + middle * shift_ref[0:1, q * freq_pad : (q + 1) * freq_pad]
        if n_tm == 2:
            sign = shift_ref[2:3, :freq_pad]
            spec_ref[:, q * freq_pad : (q + 1) * freq_pad] = part[:rows] + part[rows:] * sign
        parts.append(part)
    if n_tm != 2:
        spec_cos = jnp.zeros((rows, freq_pad), jnp.float32)
        spec_sin = jnp.zeros((rows, freq_pad), jnp.float32)
        for m in range(n_tm):
            part_cos, part_sin = (part[m * rows : (m + 1) * rows] for part in parts)
            shift_cos = shift_ref[1 + m : 2 + m, :freq_pad]
            shift_sin = shift_ref[1 + n_tm + m : 2 + n_tm + m, :freq_pad]
            spec_cos += part_cos * shift_cos - part_sin * shift_sin
            spec_sin += part_sin * shift_cos + part_cos * shift_sin
        spec_ref[:, :freq_pad] = spec_cos
        spec_ref[:, freq_pad:] = spec_sin
    turn_cos, turn_sin = surrogate_turns(frames, last_freq, phases, place)
    turn_ref[pl.ds(0, surr), :] = turn_cos
    turn_ref[pl.ds(surr, surr), :] = turn_sin
    cols_copy.wait()


def raise_top(top, rot, cols_ref):
    for j in range(cols_ref.shape[0]):
        scores = jnp.abs(jnp.dot(rot, cols_ref[j], preferred_element_type=jnp.float32))
        for part in range(0, TILE, LANES):
            top = jnp.maximum(top, scores[:, part : part + LANES])
    return top


def row_peaks(top, scale_ref, surr):
    rows = scale_ref.shape[0]
    peaks = [
        jnp.max((top[s * rows : (s + 1) * rows] * scale_ref[:, s : s + 1]).T, axis=0, keepdims=True)
        for s in range(surr)
    ]
    return jnp.concatenate(peaks, axis=0)


def first_score_kernel(
    frames, last_freq, spec_ref, turn_ref, near_ref, cols_hbm, peak_ref, far_ref, rot_ref, scale_ref, sem
):
    copy = start_copy(cols_hbm.at[pl.ds(near_ref.shape[0], far_ref.shape[0])], far_ref, sem)
    rotate(frames, last_freq, spec_ref, turn_ref, rot_ref, scale_ref)
    rot = rot_ref[...]
    top = raise_top(jnp.zeros((rot.shape[0], LANES), jnp.float32), rot, near_ref)
    copy.wait()
    peak_ref[...] = row_peaks(raise_top(top, rot, far_ref), scale_ref, peak_ref.shape[0])


def second_score_kernel(
    frames, last_freq, spec_ref, turn_ref, near_ref, far_ref, first_ref, own_ref, best_ref,
    rot_ref, scale_ref,
):
    rotate(frames, last_freq, spec_ref, turn_ref, rot_ref, scale_ref)
    rot = rot_ref[...]
    top = raise_top(jnp.zeros((rot.shape[0], LANES), jnp.float32), rot, near_ref)
    peaks = row_peaks(raise_top(top, rot, far_ref), scale_ref, first_ref.shape[0])
    first = first_ref[...]
    lane = lax.axis_index("lane")
    own_ref[lane] = first
    own_ref[1 - lane] = peaks
    best = jnp.max(jnp.maximum(first, peaks), axis=1, keepdims=True)
    lane_of = lax.broadcasted_iota(jnp.int32, (1, 1, best_ref.shape[2]), 2)
    row = jnp.zeros(lane_of.shape, jnp.float32)
    for s in range(best.shape[0]):
        row = jnp.where(lane_of == s, best[s : s + 1].reshape(1, 1, 1), row)
    best_ref[...] = jnp.broadcast_to(row, best_ref.shape)


def tm_exchange(value, n_tm):
    if n_tm == 2:
        other = lax.ppermute(value, "tm", [(0, 1), (1, 0)])
        first = lax.axis_index("tm") == 0
        return jnp.stack([jnp.where(first, value, other), jnp.where(first, other, value)])
    return lax.all_gather(value, "tm")


def lane_groups(n_grp, n_lane, n_tm):
    index = np.arange(n_grp * n_lane * n_tm).reshape(n_grp, n_lane, n_tm)
    return [index[:: 1 - 2 * lane, lane].T.reshape(-1).tolist() for lane in range(n_lane)]


def in_hbm(array):
    return pltpu.with_memory_space_constraint(array, pltpu.HBM)


def body(dims, series, slab_series, phase_index):
    n_grp, n_lane, n_tm = dims
    frames, columns = series.shape
    share, verts = slab_series.shape
    surr = phase_index.shape[0]
    freqs = phase_index.shape[1] * n_tm
    row_share = verts // n_tm
    rows = n_grp * row_share
    share_pad = round_up(phase_lane(share) + phase_chunks(freqs // n_tm, rows) * surr, LANES)
    half_pad = round_up(frames // 2, LANES)
    order = Order(freqs)
    last_freq = int(np.argmax(order.freq))
    points = 2 * order.pad
    limits = pltpu.CompilerParams(vmem_limit_bytes=24 * 2**20)

    codes = pl.pallas_call(
        functools.partial(encode_kernel, share, rows),
        out_shape=pltpu.VMEM((n_tm, n_grp, row_share, share_pad), jnp.int16),
        in_specs=[VMEM] * 2,
        out_specs=VMEM,
        compiler_params=limits,
    )(in_hbm(slab_series.T), in_hbm(phase_index))
    codes = codes.reshape(n_tm * n_grp, row_share, share_pad)
    received = lax.all_to_all(
        codes, ("grp", "lane", "tm"), 0, 0, tiled=True,
        axis_index_groups=lane_groups(n_grp, n_lane, n_tm),
    )

    n_tiles = columns // TILE
    col_high, col_low = column_tables(frames, order)
    cols = pl.pallas_call(
        column_kernel,
        out_shape=pltpu.HBM((n_tiles, points, TILE), jnp.bfloat16),
        in_specs=[HBM] * 3,
        out_specs=HBM,
        scratch_shapes=[
            pltpu.VMEM((n_tiles, frames, TILE), jnp.bfloat16),
            pltpu.VMEM(col_high.shape, jnp.bfloat16),
            pltpu.VMEM(col_low.shape, FLOAT8),
            pltpu.VMEM((n_tiles, points, TILE), jnp.bfloat16),
        ]
        + [pltpu.VMEM((2, half_pad, TILE), jnp.bfloat16)] * 2
        + [pltpu.VMEM((2, 2 * half_pad, TILE), FLOAT8)] * 2
        + [pltpu.SemaphoreType.DMA((n_tiles + 2,)), pltpu.SemaphoreType.DMA((n_tiles + 3,))],
        compiler_params=limits,
        cost_estimate=pl.CostEstimate(
            flops=6 * order.pad * frames * columns, transcendentals=0, bytes_accessed=0
        ),
    )(in_hbm(series), in_hbm(col_high), in_hbm(col_low))

    received, cols = lax.optimization_barrier((received, cols))
    high, low, shift = slab_tables(frames, share, share_pad, n_tm, order)
    place = placement(order, freqs, n_tm, rows)
    n_near = n_tiles // 2
    rot_shape = pltpu.VMEM((surr * rows, points), jnp.bfloat16)
    spec, turn, near = pl.pallas_call(
        functools.partial(spectrum_kernel, share, frames, last_freq, freqs // n_tm),
        out_shape=(
            jax.ShapeDtypeStruct((rows, points), jnp.float32),
            jax.ShapeDtypeStruct((2 * surr, order.pad), jnp.float32),
            pltpu.VMEM((n_near, points, TILE), jnp.bfloat16),
        ),
        in_specs=[VMEM] + [HBM] * 4 + [VMEM],
        out_specs=(VMEM,) * 3,
        scratch_shapes=[
            pltpu.VMEM(high.shape, jnp.bfloat16),
            pltpu.VMEM(low.shape, FLOAT8),
            pltpu.VMEM(place.shape, FLOAT8),
            pltpu.SemaphoreType.DMA((6,)),
        ],
        compiler_params=limits,
        cost_estimate=pl.CostEstimate(
            flops=4 * points * n_tm * share_pad * rows, transcendentals=0, bytes_accessed=0
        ),
    )(
        received.reshape(n_tm, rows, share_pad),
        in_hbm(high), in_hbm(low), in_hbm(place), in_hbm(cols), shift,
    )
    other = lax.ppermute(spec, "lane", [(i, (i + 1) % n_lane) for i in range(n_lane)])
    score_cost = pl.CostEstimate(
        flops=2 * points * surr * rows * columns, transcendentals=0, bytes_accessed=0
    )
    first, far = pl.pallas_call(
        functools.partial(first_score_kernel, frames, last_freq),
        out_shape=(
            jax.ShapeDtypeStruct((surr, rows), jnp.float32),
            pltpu.VMEM((n_tiles - n_near, points, TILE), jnp.bfloat16),
        ),
        in_specs=[VMEM] * 3 + [HBM],
        out_specs=(VMEM, VMEM),
        scratch_shapes=[rot_shape, pltpu.VMEM((rows, surr), jnp.float32), pltpu.SemaphoreType.DMA],
        compiler_params=limits,
        cost_estimate=score_cost,
    )(spec, turn, near, in_hbm(cols))
    n_dev = n_grp * n_lane * n_tm
    own, best = pl.pallas_call(
        functools.partial(second_score_kernel, frames, last_freq),
        out_shape=(
            jax.ShapeDtypeStruct((2, surr, rows), jnp.float32),
            jax.ShapeDtypeStruct((n_dev, 1, LANES), jnp.float32),
        ),
        in_specs=[VMEM] * 5,
        out_specs=(VMEM, VMEM),
        scratch_shapes=[rot_shape, pltpu.VMEM((rows, surr), jnp.float32)],
        compiler_params=limits,
        cost_estimate=score_cost,
    )(other, turn, near, far, first)
    every = lax.all_to_all(best, ("grp", "lane", "tm"), 0, 0, tiled=True)
    peak_all = jnp.max(every, axis=(0, 1))[:surr]

    both = tm_exchange(own[:n_lane], n_tm).reshape(n_tm, n_lane, surr, n_grp, row_share)
    both = jnp.concatenate([both[:, :1], both[:, 1:, :, ::-1]], axis=1)
    tile_peak = jnp.transpose(both, (2, 3, 1, 0, 4)).reshape(surr, -1, 1)
    return tile_peak, peak_all


def solution(mesh):
    n_col, n_tm = mesh.shape["col"], mesh.shape["tm"]
    n_lane = 2 if n_col % 2 == 0 else 1
    dims = (n_col // n_lane, n_lane, n_tm)
    split = Mesh(mesh.devices.reshape(dims), ("grp", "lane", "tm"))
    col = ("grp", "lane")
    return jax.shard_map(
        functools.partial(body, dims),
        mesh=split,
        in_specs=(P(None, col), P("tm", col), P(None, "tm")),
        out_specs=(P(None, None, col), P()),
        check_vma=False,
    )
```

```python
import functools
import math

import jax
import jax.numpy as jnp
import ml_dtypes
import numpy as np
from jax import lax
from jax.experimental import pallas as pl
from jax.experimental.pallas import tpu as pltpu
from jax.sharding import Mesh, PartitionSpec as P

EPSILON = 1e-06
LANES = 128
CODE_TOP = 32767.0
LOW_SCALE = 2.0**14
COARSE_SCALE = 2.0**6
CODE_SCALE = COARSE_SCALE / LOW_SCALE
COL_SCALE = 2.0**8
FLOAT8 = jnp.float8_e4m3fn
VMEM = pl.BlockSpec(memory_space=pltpu.VMEM)
HBM = pl.BlockSpec(memory_space=pltpu.HBM)
TILE = 2 * LANES


def round_up(value, unit):
    return -(-value // unit) * unit


def split_table(table, axis, low_scale, coarse_scale):
    high = table.astype(ml_dtypes.bfloat16)
    low = (table - high.astype(np.float64)) * low_scale
    low = np.concatenate([low, table * coarse_scale], axis=axis).astype(ml_dtypes.float8_e4m3fn)
    return jnp.asarray(np.ascontiguousarray(high)), jnp.asarray(np.ascontiguousarray(low))


class Order:
    def __init__(self, freqs):
        self.half = round_up(-(-freqs // 2), 16)
        self.pad = round_up(2 * self.half, LANES)
        self.freq = np.zeros(self.pad, np.int64)
        self.freq[: freqs // 2] = np.arange(2, freqs + 1, 2)
        self.freq[self.half : self.half + freqs - freqs // 2] = np.arange(1, freqs + 1, 2)
        self.used = self.freq > 0

    def wave(self, points, frames):
        angles = (self.freq[:, None] * points[None, :] % frames) * (2.0 * math.pi / frames)
        return np.stack([np.cos(angles), np.sin(angles)]) * self.used[:, None]


def pad_last(array, size):
    return np.pad(array, [(0, 0)] * (array.ndim - 1) + [(0, size - array.shape[-1])])


def column_tables(frames, order):
    half_pad = round_up(frames // 2, LANES)
    wave = pad_last(order.wave(np.arange(frames // 2), frames), half_pad)[:, : 2 * order.half]
    wave = wave.reshape(2, 2, order.half, half_pad).transpose(1, 0, 2, 3)
    return split_table(wave.reshape(2, 2 * order.half, half_pad) * COL_SCALE, 2, 1.0, 1.0)


def slab_tables(frames, share, share_pad, n_tm, order):
    wave = pad_last(order.wave(np.arange(share), frames), share_pad).transpose(0, 2, 1)
    high, low = split_table(wave, 1, LOW_SCALE, COARSE_SCALE)
    sums = np.concatenate([wave[0].sum(axis=0), wave[1].sum(axis=0)])
    shift = order.wave(np.arange(n_tm) * share, frames).transpose(0, 2, 1)
    shift = np.concatenate([shift, shift], axis=2).reshape(2 * n_tm, 2 * order.pad)
    return high, low, jnp.asarray(np.concatenate([sums[None], shift]), jnp.float32)


def placement(order, freqs, n_tm, rows):
    share = freqs // n_tm
    share_pad = round_up(share, rows)
    index = order.freq - 1
    row = index // share * share_pad + index % share
    table = np.zeros((n_tm * share_pad, order.pad), ml_dtypes.float8_e4m3fn)
    table[row[order.used], np.nonzero(order.used)[0]] = 1.0
    return jnp.asarray(table)


def split_digits(value):
    scaled = value * 16.0
    first = scaled.astype(jnp.int32)
    rest = (scaled - first.astype(jnp.float32)) * 32768.0
    second = rest.astype(jnp.int32)
    third = ((rest - second.astype(jnp.float32)) * 32768.0).astype(jnp.int32)
    return first, second, third


def join_digits(first, second, third):
    return (
        first.astype(jnp.float32) * 2.0**-4
        + second.astype(jnp.float32) * 2.0**-19
        + third.astype(jnp.float32) * 2.0**-34
    )


def phase_lane(share):
    return round_up(share + 6, 8)


def phase_chunks(freq_share, rows):
    return -(-freq_share // rows)


def encode_kernel(share, rows, slab_ref, phase_ref, code_ref):
    values = slab_ref[...]
    verts = values.shape[0]
    n_tm, n_grp, row_share, share_pad = code_ref.shape
    highest = jnp.max(values, axis=1, keepdims=True)
    lowest = jnp.min(values, axis=1, keepdims=True)
    middle_digits = split_digits((highest + lowest) * 0.5)
    middle = join_digits(*middle_digits)
    offset = values - middle
    top_digits = split_digits(jnp.maximum(highest - middle, middle - lowest))
    step = join_digits(*top_digits) * (1.0 / CODE_TOP)
    inverse = jnp.where(step > 0.0, 1.0 / jnp.where(step > 0.0, step, 1.0), 0.0)
    codes = jnp.clip(jnp.round(offset * inverse), -CODE_TOP, CODE_TOP).astype(jnp.int32)
    codes = jnp.concatenate(
        [codes, jnp.zeros((verts, share_pad - share), jnp.int32)], axis=1
    )
    edge = share_pad - LANES
    tail = codes[:, edge:]
    lane = lax.broadcasted_iota(jnp.int32, (verts, LANES), 1) + (edge - share)
    for place, digit in enumerate(top_digits + middle_digits):
        tail = jnp.where(lane == place, digit, tail)

    surr, freq_share = phase_ref.shape
    chunks = phase_chunks(freq_share, rows)
    phase = phase_ref[...].astype(jnp.float32)
    phase = jnp.concatenate(
        [phase, jnp.zeros((surr, chunks * rows - freq_share), jnp.float32)], axis=1
    )
    phase = jnp.concatenate([phase[:, c * rows : (c + 1) * rows] for c in range(chunks)], axis=0)
    above = phase_lane(share) % LANES
    phase = jnp.concatenate(
        [
            jnp.zeros((above, rows), jnp.float32),
            phase,
            jnp.zeros((LANES - above - chunks * surr, rows), jnp.float32),
        ],
        axis=0,
    )
    group = lax.axis_index("grp")
    place = jnp.where(lax.axis_index("lane") == 0, group, n_grp - 1 - group)
    phase = pltpu.roll(phase, rows - place * row_share, 1).T[:row_share]
    phase = jnp.concatenate([phase.astype(jnp.int32)] * n_tm, axis=0)
    codes = jnp.concatenate([codes[:, :edge], tail + phase], axis=1)
    for m in range(n_tm):
        block = codes[m * row_share : (m + 1) * row_share].astype(jnp.int16)
        for g in range(n_grp):
            code_ref[m, g] = block


def start_copy(source, target, sem):
    copy = pltpu.make_async_copy(source, target, sem)
    copy.start()
    return copy


def wait_all(copies):
    for copy in copies:
        copy.wait()


def column_kernel(
    series_hbm, high_hbm, low_hbm, slab_low_hbm, out_hbm, slab_low_ref,
    series, high, low, out, normed_0, normed_1, coarse_0, coarse_1, load_sems, store_sems,
):
    n_tiles, frames, _ = series.shape
    half = frames // 2
    half_pad = high.shape[2]
    freq_half = high.shape[1] // 2
    freq_pad = out.shape[1] // 2
    gap = freq_pad - 2 * freq_half
    normed_refs, coarse_refs = (normed_0, normed_1), (coarse_0, coarse_1)

    def load_tile(j):
        return start_copy(series_hbm.at[:, pl.ds(j * TILE, TILE)], series.at[j], load_sems.at[j])

    tile_copies = [load_tile(0)]
    table_copies = [
        start_copy(high_hbm, high, load_sems.at[n_tiles]),
        start_copy(low_hbm, low, load_sems.at[n_tiles + 1]),
    ]
    tile_copies += [load_tile(j) for j in range(1, n_tiles)]

    def normalize(j):
        normed_ref, coarse_ref = normed_refs[j % 2], coarse_refs[j % 2]
        values = series[j].astype(jnp.float32)
        centered = values - jnp.sum(values, axis=0, keepdims=True) * (1.0 / frames)
        total = jnp.sum(centered * centered, axis=0, keepdims=True)
        normed = centered * (lax.rsqrt(total + EPSILON) * COL_SCALE)
        first, second = (
            jnp.concatenate([part, jnp.zeros((half_pad - half, TILE), jnp.float32)], axis=0).astype(
                jnp.bfloat16
            )
            for part in (normed[:half], normed[half:])
        )
        for parity, other in enumerate((second, -second)):
            rounded = first + other
            added = rounded - first
            rest = (first - (rounded - added)) + (other - added)
            normed_ref[parity] = rounded
            coarse_ref[parity, pl.ds(0, half_pad), :] = rounded.astype(FLOAT8)
            coarse_ref[parity, pl.ds(half_pad, half_pad), :] = rest.astype(FLOAT8)

    tile_copies[0].wait()
    normalize(0)
    wait_all(table_copies + tile_copies[1:2])
    stores = []
    if gap:
        for q in range(2):
            span = pl.ds(q * freq_pad + 2 * freq_half, gap)
            out[:, span, :] = jnp.zeros((n_tiles, gap, TILE), jnp.bfloat16)
    for j in range(n_tiles):
        if j == 1:
            wait_all(tile_copies[2:])
            slab_copy = start_copy(slab_low_hbm, slab_low_ref, load_sems.at[n_tiles + 2])
        if j + 1 < n_tiles:
            normalize(j + 1)
        for parity in range(2):
            sums = jnp.dot(
                high[parity], normed_refs[j % 2][parity], preferred_element_type=jnp.float32
            )
            rest = jnp.dot(
                low[parity], coarse_refs[j % 2][parity], preferred_element_type=jnp.float32
            )
            sums = (sums + rest).astype(jnp.bfloat16)
            for q in range(2):
                span = pl.ds(q * freq_pad + parity * freq_half, freq_half)
                out[j, span, :] = sums[q * freq_half : (q + 1) * freq_half]
                if j + 1 == n_tiles:
                    start = q * freq_pad + parity * freq_half
                    part = pl.ds(start, freq_half + parity * gap)
                    place = n_tiles - 1 + 2 * parity + q
                    stores.append(start_copy(out.at[j, part], out_hbm.at[j, part], store_sems.at[place]))
        if j + 1 < n_tiles:
            stores.append(start_copy(out.at[j], out_hbm.at[j], store_sems.at[j]))
    wait_all([slab_copy] + stores)


def surrogate_turns(frames, last_freq, phases, place_ref):
    surr = phases[0].shape[0]
    freq_pad = place_ref.shape[1]
    digits = []
    for phase in phases:
        parts = [phase >> 8, (phase >> 4) & 15, phase & 15]
        digits.append(jnp.concatenate(parts, axis=0).astype(jnp.float32))
    digits = jnp.concatenate(digits, axis=1).astype(FLOAT8)
    placed = jnp.dot(digits, place_ref[...], preferred_element_type=jnp.float32)
    turn = placed[:surr] * 256.0 + placed[surr : 2 * surr] * 16.0 + placed[2 * surr :]
    freq = lax.broadcasted_iota(jnp.int32, (1, freq_pad), 1)
    weight = jnp.where(freq == last_freq, 1.0 / frames, 2.0 / frames)
    cos, sin = turn_waves(frames, turn)
    return cos * weight, sin * weight


def turn_waves(frames, turn):
    quarter = frames / 4
    quadrant = jnp.floor(turn * (1.0 / quarter) + 0.5)
    x = (turn - quadrant * quarter) * (2.0 * math.pi / frames)
    y = x * x
    cos = 1.0 + y * (-1 / 2 + y * (1 / 24 + y * (-1 / 720 + y * (1 / 40320 - y * (1 / 3628800)))))
    sin = x * (1.0 + y * (-1 / 6 + y * (1 / 120 + y * (-1 / 5040 + y * (1 / 362880)))))
    odd = (quadrant == 1.0) | (quadrant == 3.0)
    left = (quadrant == 1.0) | (quadrant == 2.0)
    down = (quadrant == 2.0) | (quadrant == 3.0)
    near = jnp.where(odd, sin, cos)
    far = jnp.where(odd, cos, sin)
    return jnp.where(left, -near, near), jnp.where(down, -far, far)


def rotate(frames, last_freq, spec_ref, turn_ref, rot_ref, scale_ref):
    rows = spec_ref.shape[0]
    surr, freq_pad = turn_ref.shape[0] // 2, turn_ref.shape[1]
    spec_cos = spec_ref[:, :freq_pad]
    spec_sin = spec_ref[:, freq_pad:]
    freq = lax.broadcasted_iota(jnp.int32, (1, freq_pad), 1)
    pair = jnp.where(freq != last_freq, (2.0 / frames) ** 2 * (frames / 2.0), 0.0)
    common = jnp.sum((spec_cos * spec_cos + spec_sin * spec_sin) * pair, axis=1, keepdims=True)
    block = last_freq // LANES * LANES
    last = jnp.where(freq[:, block : block + LANES] == last_freq, float(frames), 0.0)
    for s in range(surr):
        cos_row = turn_ref[pl.ds(s, 1), :]
        sin_row = turn_ref[pl.ds(surr + s, 1), :]
        rot_real = spec_cos * cos_row + spec_sin * sin_row
        rot_imag = spec_cos * sin_row - spec_sin * cos_row
        at_last = rot_real[:, block : block + LANES]
        energy = common + jnp.sum(at_last * at_last * last, axis=1, keepdims=True)
        scale_ref[:, s : s + 1] = lax.rsqrt(energy + EPSILON) * (math.sqrt(frames) / COL_SCALE**2)
        span = pl.ds(s * rows, rows)
        rot_ref[span, :freq_pad] = rot_real.astype(jnp.bfloat16)
        rot_ref[span, freq_pad:] = (-rot_imag).astype(jnp.bfloat16)


def spectrum_kernel(
    share, frames, last_freq, freq_share,
    codes_ref, low, high_hbm, place_hbm, cols_hbm, shift_ref,
    spec_ref, turn_ref, cols_ref,
    high, place, sems,
):
    n_tm, rows, share_pad = codes_ref.shape
    freq_pad = high.shape[2]
    copies = [start_copy(high_hbm.at[q], high.at[q], sems.at[q]) for q in range(2)]
    place_copy = start_copy(place_hbm, place, sems.at[2])
    cols_copy = start_copy(cols_hbm.at[pl.ds(0, cols_ref.shape[0])], cols_ref, sems.at[3])
    codes = codes_ref[...].reshape(n_tm * rows, share_pad).astype(jnp.int32)
    upper = ((codes + 128) >> 8) << 8
    lower = (codes - upper).astype(jnp.float32)
    upper = upper.astype(jnp.float32)
    coarse = jnp.concatenate([upper * CODE_SCALE, lower], axis=1).astype(FLOAT8)
    upper = upper.astype(jnp.bfloat16)
    digits = [codes[:, share + p : share + p + 1] for p in range(6)]
    step = join_digits(*digits[:3]) * (1.0 / CODE_TOP)
    middle = join_digits(*digits[3:])
    surr = turn_ref.shape[0] // 2
    chunks = phase_chunks(freq_share, rows)
    above = phase_lane(share) % LANES
    phases = []
    for m in range(n_tm):
        block = codes[m * rows : (m + 1) * rows, share_pad - LANES :].astype(jnp.float32).T
        block = block[above : above + round_up(chunks * surr, 8)].astype(jnp.int32)
        parts = [block[c * surr : (c + 1) * surr] for c in range(chunks)]
        phases.append(jnp.concatenate(parts, axis=1))
    parts = []
    for q in range(2):
        wait_all([copies[q]] + [place_copy] * q)
        part = jnp.dot(upper, high[q], preferred_element_type=jnp.float32)
        part += jnp.dot(coarse, low[q], preferred_element_type=jnp.float32) * (1.0 / COARSE_SCALE)
        part = part * step + middle * shift_ref[0:1, q * freq_pad : (q + 1) * freq_pad]
        if n_tm == 2:
            sign = shift_ref[2:3, :freq_pad]
            spec_ref[:, q * freq_pad : (q + 1) * freq_pad] = part[:rows] + part[rows:] * sign
        parts.append(part)
    if n_tm != 2:
        spec_cos = jnp.zeros((rows, freq_pad), jnp.float32)
        spec_sin = jnp.zeros((rows, freq_pad), jnp.float32)
        for m in range(n_tm):
            part_cos, part_sin = (part[m * rows : (m + 1) * rows] for part in parts)
            shift_cos = shift_ref[1 + m : 2 + m, :freq_pad]
            shift_sin = shift_ref[1 + n_tm + m : 2 + n_tm + m, :freq_pad]
            spec_cos += part_cos * shift_cos - part_sin * shift_sin
            spec_sin += part_sin * shift_cos + part_cos * shift_sin
        spec_ref[:, :freq_pad] = spec_cos
        spec_ref[:, freq_pad:] = spec_sin
    turn_cos, turn_sin = surrogate_turns(frames, last_freq, phases, place)
    turn_ref[pl.ds(0, surr), :] = turn_cos
    turn_ref[pl.ds(surr, surr), :] = turn_sin
    cols_copy.wait()


def raise_top(top, rot, cols_ref):
    for j in range(cols_ref.shape[0]):
        scores = jnp.abs(jnp.dot(rot, cols_ref[j], preferred_element_type=jnp.float32))
        for part in range(0, TILE, LANES):
            top = jnp.maximum(top, scores[:, part : part + LANES])
    return top


def row_peaks(top, scale_ref, surr):
    rows = scale_ref.shape[0]
    peaks = [
        jnp.max((top[s * rows : (s + 1) * rows] * scale_ref[:, s : s + 1]).T, axis=0, keepdims=True)
        for s in range(surr)
    ]
    return jnp.concatenate(peaks, axis=0)


def first_score_kernel(
    frames, last_freq, spec_ref, turn_ref, near_ref, cols_hbm, peak_ref, far_ref, rot_ref, scale_ref, sem
):
    copy = start_copy(cols_hbm.at[pl.ds(near_ref.shape[0], far_ref.shape[0])], far_ref, sem)
    rotate(frames, last_freq, spec_ref, turn_ref, rot_ref, scale_ref)
    rot = rot_ref[...]
    top = raise_top(jnp.zeros((rot.shape[0], LANES), jnp.float32), rot, near_ref)
    copy.wait()
    peak_ref[...] = row_peaks(raise_top(top, rot, far_ref), scale_ref, peak_ref.shape[0])


def second_score_kernel(
    frames, last_freq, spec_ref, turn_ref, near_ref, far_ref, first_ref, own_ref, best_ref,
    rot_ref, scale_ref,
):
    rotate(frames, last_freq, spec_ref, turn_ref, rot_ref, scale_ref)
    rot = rot_ref[...]
    top = raise_top(jnp.zeros((rot.shape[0], LANES), jnp.float32), rot, near_ref)
    peaks = row_peaks(raise_top(top, rot, far_ref), scale_ref, first_ref.shape[0])
    first = first_ref[...]
    lane = lax.axis_index("lane")
    own_ref[lane] = first
    own_ref[1 - lane] = peaks
    best = jnp.max(jnp.maximum(first, peaks), axis=1, keepdims=True)
    lane_of = lax.broadcasted_iota(jnp.int32, (1, 1, best_ref.shape[2]), 2)
    row = jnp.zeros(lane_of.shape, jnp.float32)
    for s in range(best.shape[0]):
        row = jnp.where(lane_of == s, best[s : s + 1].reshape(1, 1, 1), row)
    best_ref[...] = jnp.broadcast_to(row, best_ref.shape)


def tm_exchange(value, n_tm):
    if n_tm == 2:
        other = lax.ppermute(value, "tm", [(0, 1), (1, 0)])
        first = lax.axis_index("tm") == 0
        return jnp.stack([jnp.where(first, value, other), jnp.where(first, other, value)])
    return lax.all_gather(value, "tm")


def lane_groups(n_grp, n_lane, n_tm):
    index = np.arange(n_grp * n_lane * n_tm).reshape(n_grp, n_lane, n_tm)
    return [index[:: 1 - 2 * lane, lane].T.reshape(-1).tolist() for lane in range(n_lane)]


def in_hbm(array):
    return pltpu.with_memory_space_constraint(array, pltpu.HBM)


def body(dims, series, slab_series, phase_index):
    n_grp, n_lane, n_tm = dims
    frames, columns = series.shape
    share, verts = slab_series.shape
    surr = phase_index.shape[0]
    freqs = phase_index.shape[1] * n_tm
    row_share = verts // n_tm
    rows = n_grp * row_share
    share_pad = round_up(phase_lane(share) + phase_chunks(freqs // n_tm, rows) * surr, LANES)
    half_pad = round_up(frames // 2, LANES)
    order = Order(freqs)
    last_freq = int(np.argmax(order.freq))
    points = 2 * order.pad
    limits = pltpu.CompilerParams(vmem_limit_bytes=24 * 2**20)

    codes = pl.pallas_call(
        functools.partial(encode_kernel, share, rows),
        out_shape=pltpu.VMEM((n_tm, n_grp, row_share, share_pad), jnp.int16),
        in_specs=[VMEM] * 2,
        out_specs=VMEM,
        compiler_params=limits,
    )(in_hbm(slab_series.T), in_hbm(phase_index))
    codes = codes.reshape(n_tm * n_grp, row_share, share_pad)
    received = lax.all_to_all(
        codes, ("grp", "lane", "tm"), 0, 0, tiled=True,
        axis_index_groups=lane_groups(n_grp, n_lane, n_tm),
    )

    n_tiles = columns // TILE
    col_high, col_low = column_tables(frames, order)
    high, low, shift = slab_tables(frames, share, share_pad, n_tm, order)
    cols, low = pl.pallas_call(
        column_kernel,
        out_shape=(
            pltpu.HBM((n_tiles, points, TILE), jnp.bfloat16),
            pltpu.VMEM(low.shape, FLOAT8),
        ),
        in_specs=[HBM] * 4,
        out_specs=(HBM, VMEM),
        scratch_shapes=[
            pltpu.VMEM((n_tiles, frames, TILE), jnp.bfloat16),
            pltpu.VMEM(col_high.shape, jnp.bfloat16),
            pltpu.VMEM(col_low.shape, FLOAT8),
            pltpu.VMEM((n_tiles, points, TILE), jnp.bfloat16),
        ]
        + [pltpu.VMEM((2, half_pad, TILE), jnp.bfloat16)] * 2
        + [pltpu.VMEM((2, 2 * half_pad, TILE), FLOAT8)] * 2
        + [pltpu.SemaphoreType.DMA((n_tiles + 3,)), pltpu.SemaphoreType.DMA((n_tiles + 3,))],
        compiler_params=limits,
        cost_estimate=pl.CostEstimate(
            flops=6 * order.pad * frames * columns, transcendentals=0, bytes_accessed=0
        ),
    )(in_hbm(series), in_hbm(col_high), in_hbm(col_low), in_hbm(low))

    received, cols = lax.optimization_barrier((received, cols))
    place = placement(order, freqs, n_tm, rows)
    n_near = n_tiles // 2
    rot_shape = pltpu.VMEM((surr * rows, points), jnp.bfloat16)
    spec, turn, near = pl.pallas_call(
        functools.partial(spectrum_kernel, share, frames, last_freq, freqs // n_tm),
        out_shape=(
            jax.ShapeDtypeStruct((rows, points), jnp.float32),
            jax.ShapeDtypeStruct((2 * surr, order.pad), jnp.float32),
            pltpu.VMEM((n_near, points, TILE), jnp.bfloat16),
        ),
        in_specs=[VMEM] * 2 + [HBM] * 3 + [VMEM],
        out_specs=(VMEM,) * 3,
        scratch_shapes=[
            pltpu.VMEM(high.shape, jnp.bfloat16),
            pltpu.VMEM(place.shape, FLOAT8),
            pltpu.SemaphoreType.DMA((4,)),
        ],
        compiler_params=limits,
        cost_estimate=pl.CostEstimate(
            flops=4 * points * n_tm * share_pad * rows, transcendentals=0, bytes_accessed=0
        ),
    )(
        received.reshape(n_tm, rows, share_pad),
        low, in_hbm(high), in_hbm(place), in_hbm(cols), shift,
    )
    other = lax.ppermute(spec, "lane", [(i, (i + 1) % n_lane) for i in range(n_lane)])
    score_cost = pl.CostEstimate(
        flops=2 * points * surr * rows * columns, transcendentals=0, bytes_accessed=0
    )
    first, far = pl.pallas_call(
        functools.partial(first_score_kernel, frames, last_freq),
        out_shape=(
            jax.ShapeDtypeStruct((surr, rows), jnp.float32),
            pltpu.VMEM((n_tiles - n_near, points, TILE), jnp.bfloat16),
        ),
        in_specs=[VMEM] * 3 + [HBM],
        out_specs=(VMEM, VMEM),
        scratch_shapes=[rot_shape, pltpu.VMEM((rows, surr), jnp.float32), pltpu.SemaphoreType.DMA],
        compiler_params=limits,
        cost_estimate=score_cost,
    )(spec, turn, near, in_hbm(cols))
    n_dev = n_grp * n_lane * n_tm
    own, best = pl.pallas_call(
        functools.partial(second_score_kernel, frames, last_freq),
        out_shape=(
            jax.ShapeDtypeStruct((2, surr, rows), jnp.float32),
            jax.ShapeDtypeStruct((n_dev, 1, LANES), jnp.float32),
        ),
        in_specs=[VMEM] * 5,
        out_specs=(VMEM, VMEM),
        scratch_shapes=[rot_shape, pltpu.VMEM((rows, surr), jnp.float32)],
        compiler_params=limits,
        cost_estimate=score_cost,
    )(other, turn, near, far, first)
    every = lax.all_to_all(best, ("grp", "lane", "tm"), 0, 0, tiled=True)
    peak_all = jnp.max(every, axis=(0, 1))[:surr]

    both = tm_exchange(own[:n_lane], n_tm).reshape(n_tm, n_lane, surr, n_grp, row_share)
    both = jnp.concatenate([both[:, :1], both[:, 1:, :, ::-1]], axis=1)
    tile_peak = jnp.transpose(both, (2, 3, 1, 0, 4)).reshape(surr, -1, 1)
    return tile_peak, peak_all


def solution(mesh):
    n_col, n_tm = mesh.shape["col"], mesh.shape["tm"]
    n_lane = 2 if n_col % 2 == 0 else 1
    dims = (n_col // n_lane, n_lane, n_tm)
    split = Mesh(mesh.devices.reshape(dims), ("grp", "lane", "tm"))
    col = ("grp", "lane")
    return jax.shard_map(
        functools.partial(body, dims),
        mesh=split,
        in_specs=(P(None, col), P("tm", col), P(None, "tm")),
        out_specs=(P(None, None, col), P()),
        check_vma=False,
    )
```
